128 devices in a mesh: panel: 32 (over y, x, core), lag: 4 (over z).
Axes of the slice: x: 4, y: 4, z: 4, core: 2. Of those that a mesh axis runs over, the one named last changes fastest.
Arguments:
- strengths: bfloat16 [131072, 384], P(('panel', 'lag')), may hold values from -6 to 6
- incident_green: bfloat16 [32768, 128, 128], P(('panel', 'lag')), may hold values from -0.02734375 to 0.02734375
- targets: int32 [32768], P(('panel', 'lag')), may hold values from 0 to 95
- history: bfloat16 [8, 12288, 128], P('lag', 'panel'), may hold values from -6 to 6
- retarded: bfloat16 [8, 96, 16, 128, 128], P('lag', 'panel'), may hold values from -0.046875 to 0.046875
- columns: int32 [8, 96, 16], P('lag', 'panel'), may hold values from 0 to 95, all different within a row
- inverse: float32 [96, 128, 128], P('panel'), may hold values from -0.5 to 0.5
Outputs:
- solutions: bfloat16 [3, 12288, 128], P(None, 'panel')
The draws below stay inside these ranges and needn't reach their ends.
Inputs may be any that keep to these rules, and one draw needn't show every extreme that they name: `columns`: each row of a lag names 16 different column blocks.
All inputs are finite; a program needn't handle non-finite values.
Results may differ from the reference program's by a relative error of at most 0.0026.
Values may be sent and summed in bfloat16 or wider, within the bound.
A program may use at most 192 MiB of HBM per device.

```python
import math
import jax
import jax.numpy as jnp
import numpy as np
from jax import lax

BLOCK = 128
BLK_DEV = 3
CASES = 128
LAGS = 8
STEPS = 3
SG = 256
CB = 8
KNZ = 16
GPC = 32
NBLK = 96
PANELS = 12288
SRCB = 32768
CELLS = 131072
N_LAG = 4


def place_ends(array, key, least, top_value):
    longest = array.shape.index(max(array.shape))
    spots = []
    for shift in (0, 1):
        where = [jax.random.randint(jax.random.fold_in(key, axis), (), 0, length) for axis, length in enumerate(array.shape)]
        where[longest] = (where[longest] + shift) % array.shape[longest]
        spots.append(tuple(where))
    return array.at[spots[0]].set(least).at[spots[1]].set(top_value)


def block_levels(stream_key, extent, pieces, least, high):
    def one(axis_at, parts):
        draws = jax.random.uniform(jax.random.fold_in(jax.random.fold_in(stream_key, 6), axis_at), (parts,), jnp.float32, least / len(pieces), high / len(pieces))
        return jnp.repeat(jnp.exp(draws), extent[axis_at] // parts).reshape((-1,) + (1,) * (len(extent) - axis_at - 1))

    loudness = one(*pieces[0])
    for cut in pieces[1:]:
        loudness = loudness * one(*cut)
    return loudness


def rank_table(number_of, slope):
    loads = [(1 << 20) // math.isqrt(rank ** slope) + 1 for rank in range(1, number_of + 1)]
    deviation = 1 + sum(loads) // (1 << 30)
    return np.cumsum(np.array([max(1, weight // deviation) for weight in loads]))


def ranked_ids(rng, shape, amount, skew):
    grid = rank_table(amount, skew)
    pick = jax.random.randint(jax.random.fold_in(rng, 1), shape, 0, int(grid[amount - 1]))
    standing = jnp.searchsorted(jnp.asarray(grid, jnp.int32), pick, side="right")
    return jax.random.permutation(jax.random.fold_in(rng, 2), amount)[standing].astype(jnp.int32)


def picks_of(own_key, rows, amount, top, lift):
    order = jax.random.permutation(jax.random.fold_in(own_key, 1), amount)
    boost = order
    for power in range(3):
        boost = boost * boost // amount
    boost = boost * lift // amount
    lots = jax.random.randint(jax.random.fold_in(own_key, 2), (rows, amount), 0, 4096) + boost
    sure = jax.random.permutation(jax.random.fold_in(own_key, 3), rows)[jnp.arange(amount) % rows]
    lots = jnp.where(jnp.arange(rows)[:, None] == sure[None, :], 1 << 14, lots)
    score = lots * amount + jnp.arange(amount)
    return lax.top_k(score.astype(jnp.int32), top)[1].astype(jnp.int32)


def bell_draw(key, extent, deviation, limit, cuts=(), held_as=jnp.bfloat16):
    array = deviation * jax.random.normal(key, extent, jnp.float32)
    if cuts:
        array = array * block_levels(key, extent, cuts, -0.22, 0.18)
    return jnp.clip(array, -limit, limit).astype(held_as)


def setup_inputs(seed: int = 0) -> dict:
    keys = jax.random.split(jax.random.key(seed), 8)
    return {
        "strengths": bell_draw(keys[0], (CELLS, STEPS * CASES), 1.0, 6.0, ((0, 128),)),
        "incident_green": bell_draw(keys[1], (SRCB, BLOCK, BLOCK), (BLOCK * SG * N_LAG // BLK_DEV) ** -0.5, 0.02734375, ((0, 128),)),
        "targets": place_ends(ranked_ids(keys[2], (SRCB,), NBLK, 2), jax.random.fold_in(keys[2], 3), 0, NBLK - 1).astype(jnp.int32),
        "history": bell_draw(keys[3], (LAGS, PANELS, CASES), 1.0, 6.0, ((0, 4), (1, 32))),
        "retarded": bell_draw(keys[4], (LAGS, NBLK, KNZ, BLOCK, BLOCK), (BLOCK * KNZ * LAGS) ** -0.5, 0.046875, ((0, 4), (1, 32))),
        "columns": picks_of(keys[5], LAGS * NBLK, NBLK, KNZ, 0).reshape((LAGS, NBLK, KNZ)),
        "inverse": bell_draw(keys[6], (NBLK, BLOCK, BLOCK), BLOCK ** -0.5, 0.5, ((0, 32),), jnp.float32),
    }


def incident_field(strengths, incident_green, targets):
    cell_rows = strengths.reshape(-1, BLOCK, STEPS * CASES)
    count = incident_green.shape[0] // SG

    def add_piece(running, index):
        start = index * SG
        green = lax.dynamic_slice_in_dim(incident_green, start, SG, 0)
        sources = lax.dynamic_slice_in_dim(cell_rows, index * CB, CB, 0)
        green = green.reshape(CB, GPC, BLOCK, BLOCK).astype(jnp.float32)
        contrib = jnp.einsum('gibc,gcn->gibn', green, sources.astype(jnp.float32)).reshape(SG, BLOCK, STEPS * CASES)
        aimed = lax.dynamic_slice_in_dim(targets, start, SG, 0)
        return running + jax.ops.segment_sum(contrib, aimed, num_segments=NBLK), None

    initial = jnp.zeros((NBLK, BLOCK, STEPS * CASES), jnp.float32)
    summed, unused = lax.scan(add_piece, initial, jnp.arange(count, dtype=jnp.int32))
    return summed.reshape(NBLK, BLOCK, STEPS, CASES)


def reference(strengths, incident_green, targets, history, retarded, columns, inverse):
    incident = incident_field(strengths, incident_green, targets)
    past_blocks = history.reshape(LAGS, NBLK, BLOCK, CASES)
    solved = []
    for moment in range(STEPS):
        fields = []
        for lag_number in range(1, LAGS + 1):
            offset = moment - lag_number
            if offset >= 0:
                fields.append(solved[offset])
            else:
                fields.append(past_blocks[-offset - 1])
        fields = jnp.stack(fields)

        def lag_term(running, inputs):
            matrices, column_ids, field_blocks = inputs
            chosen = field_blocks[column_ids].astype(jnp.float32)
            return running + jnp.einsum('rkbc,rkcn->rbn', matrices.astype(jnp.float32), chosen), None

        start = jnp.zeros((NBLK, BLOCK, CASES), jnp.float32)
        hsum, unused = lax.scan(lag_term, start, (retarded, columns, fields))
        rhs = incident[:, :, moment, :] - hsum
        solution = jnp.einsum('rbc,rcn->rbn', inverse, rhs, precision=lax.Precision.HIGHEST).astype(jnp.bfloat16)
        solved.append(solution)
    return jnp.stack(solved).reshape(STEPS, NBLK * BLOCK, CASES)
```

```python
import functools

import jax
import jax.numpy as jnp
from jax import lax
from jax.experimental import pallas as pl
from jax.experimental.pallas import tpu as pltpu
from jax.sharding import PartitionSpec as P


def incident_kernel(per_cell, steps, targets, green, cells, out, total, sem):
    group = pl.program_id(0)
    width = green.shape[1]

    @pl.when(group == 0)
    def clear():
        total[...] = jnp.zeros_like(total)

    def add_block(i, carry):
        target = targets[group * per_cell + i]
        product = jnp.dot(green[i], cells[...], preferred_element_type=jnp.float32)
        for s in range(steps):
            total[s, target] += product[:, s * width : (s + 1) * width]
        return carry

    lax.fori_loop(0, per_cell, add_block, 0, unroll=4)

    @pl.when(group == pl.num_programs(0) - 1)
    def store():
        copies = [
            pltpu.make_async_copy(
                total.at[s], out.at[:, :, pl.ds(s * width, width)], sem.at[s]
            )
            for s in range(steps)
        ]
        for copy in copies:
            copy.start()
        for copy in copies:
            copy.wait()


def incident_partial(strengths, green, targets, all_blocks, steps):
    count, width, _ = green.shape
    cell_blocks = strengths.shape[0] // width
    per_cell = count // cell_blocks
    return pl.pallas_call(
        functools.partial(incident_kernel, per_cell, steps),
        out_shape=jax.ShapeDtypeStruct((all_blocks, width, strengths.shape[1]), jnp.float32),
        grid_spec=pltpu.PrefetchScalarGridSpec(
            num_scalar_prefetch=1,
            grid=(cell_blocks,),
            in_specs=[
                pl.BlockSpec((per_cell, width, width), lambda g, t: (g, 0, 0)),
                pl.BlockSpec((width, strengths.shape[1]), lambda g, t: (g, 0)),
            ],
            out_specs=pl.BlockSpec(memory_space=pl.ANY),
            scratch_shapes=[
                pltpu.VMEM((steps, all_blocks, width, width), jnp.float32),
                pltpu.SemaphoreType.DMA((steps,)),
            ],
        ),
        compiler_params=pltpu.CompilerParams(vmem_limit_bytes=40 * 2**20),
    )(targets, green, strengths)


def passed_along(array, axis, by):
    size = lax.axis_size(axis)
    pairs = [(i, i + by) for i in range(size) if 0 <= i + by < size]
    return lax.ppermute(array, axis, pairs)


def lag_product(matrices, column_ids, field_blocks):
    chosen = field_blocks[column_ids]
    return jnp.einsum("rkbc,rkcn->rbn", matrices, chosen, preferred_element_type=jnp.float32)


def apply_inverse(inverse, values):
    blocks = values.reshape(inverse.shape[0], inverse.shape[1], -1)
    result = jnp.einsum("rbc,rcn->rbn", inverse, blocks, precision=lax.Precision.HIGHEST)
    return result.reshape(inverse.shape[0] * inverse.shape[1], -1)


def local(strengths, incident_green, targets, history, retarded, columns, inverse):
    lag_dev = history.shape[0]
    own_rows = history.shape[1]
    cases = history.shape[2]
    width = inverse.shape[1]
    own_blocks = inverse.shape[0]
    steps = strengths.shape[1] // cases
    all_blocks = own_blocks * lax.axis_size("panel")
    partial_value = incident_partial(strengths, incident_green, targets, all_blocks, steps)
    partial_value = partial_value.reshape(all_blocks * width, steps * cases)
    incident_part = lax.psum_scatter(partial_value, "panel", scatter_dimension=0, tiled=True)
    younger = passed_along(history, "lag", 1)
    extended = jnp.concatenate([younger, history], 0)
    gathered = lax.all_gather(extended, "panel", axis=1, tiled=True)
    gathered = gathered.reshape(extended.shape[0], all_blocks, width, cases)
    leading = (lax.axis_index("lag") == 0).astype(jnp.float32)
    solved = []
    new_blocks = []
    for moment in range(steps):
        running = jnp.zeros((own_blocks, width, cases), jnp.float32)
        for lag_local in range(lag_dev):
            running = running + lag_product(
                retarded[lag_local], columns[lag_local], gathered[lag_local + steps - 1 - moment]
            )
        for lag_number in range(1, moment + 1):
            running = running + leading * lag_product(
                retarded[lag_number - 1], columns[lag_number - 1], new_blocks[moment - lag_number]
            )
        running = running.reshape(own_rows, cases)
        local_rhs = incident_part[:, moment * cases : (moment + 1) * cases] - running
        rhs_total = lax.psum(local_rhs, "lag")
        solution = apply_inverse(inverse, rhs_total).astype(jnp.bfloat16)
        solved.append(solution)
        if moment + 1 < steps:
            spread_out = lax.all_gather(solution, "panel", axis=0, tiled=True)
            new_blocks.append(spread_out.reshape(all_blocks, width, cases))
    return jnp.stack(solved)


def solution(mesh):
    placed = (
        P(("panel", "lag"), None),
        P(("panel", "lag"), None, None),
        P(("panel", "lag")),
        P("lag", "panel", None),
        P("lag", "panel", None, None, None),
        P("lag", "panel", None),
        P("panel", None, None),
    )
    return jax.shard_map(
        local, mesh=mesh, in_specs=placed, out_specs=P(None, "panel", None), check_vma=False
    )
```

```python
import functools

import jax
import jax.numpy as jnp
from jax import lax
from jax.experimental import pallas as pl
from jax.experimental.pallas import tpu as pltpu
from jax.sharding import PartitionSpec as P

MESH = pl.DeviceIdType.MESH
RING = 4
SUM = jnp.float32


def passed_along(array, axis, by):
    size = lax.axis_size(axis)
    pairs = [(i, i + by) for i in range(size) if 0 <= i + by < size]
    return lax.ppermute(array, axis, pairs)


def incident_kernel(per_cell, steps, targets, green, cells, out, total, sem):
    group = pl.program_id(0)
    width = green.shape[1]
    own_blocks = total.shape[3]
    quarter = width // RING

    @pl.when(group == 0)
    def clear():
        def one(i, carry):
            total[i // (RING * RING), i % (RING * RING)] = jnp.zeros(total.shape[2:], SUM)
            return carry

        lax.fori_loop(0, steps * RING * RING, one, 0)

    def add_block(i, carry):
        target = targets[group * per_cell + i]
        device, block = target // own_blocks, target % own_blocks
        chip, core = device // 2, device % 2
        product = jnp.dot(green[i], cells[...], preferred_element_type=SUM)
        for s in range(steps):
            total[s, chip, core, block] += product[:, s * width : (s + 1) * width]
        return carry

    lax.fori_loop(0, per_cell, add_block, 0, unroll=4)

    @pl.when(group == pl.num_programs(0) - 1)
    def store():
        copies = []
        for s in range(steps):
            for core in range(2):
                for j in range(RING):
                    copies.append(
                        pltpu.make_async_copy(
                            total.at[s, :, core, :, pl.ds(j * quarter, quarter)],
                            out.at[s, core, j],
                            sem.at[s, core, j],
                        )
                    )
        for copy in copies:
            copy.start()
        for copy in copies:
            copy.wait()


def incident_partial(strengths, green, targets, own_blocks, steps):
    count, width, _ = green.shape
    cell_blocks = strengths.shape[0] // width
    per_cell = count // cell_blocks
    chips = RING * RING
    return pl.pallas_call(
        functools.partial(incident_kernel, per_cell, steps),
        out_shape=jax.ShapeDtypeStruct(
            (steps, 2, RING, chips, own_blocks, width // RING, width), SUM
        ),
        grid_spec=pltpu.PrefetchScalarGridSpec(
            num_scalar_prefetch=1,
            grid=(cell_blocks,),
            in_specs=[
                pl.BlockSpec((per_cell, width, width), lambda g, t: (g, 0, 0)),
                pl.BlockSpec((width, strengths.shape[1]), lambda g, t: (g, 0)),
            ],
            out_specs=pl.BlockSpec(memory_space=pl.ANY),
            scratch_shapes=[
                pltpu.VMEM((steps, chips, 2, own_blocks, width, width), SUM),
                pltpu.SemaphoreType.DMA((steps, 2, RING)),
            ],
        ),
        compiler_params=pltpu.CompilerParams(vmem_limit_bytes=40 * 2**20),
    )(targets, green, strengths)


def add_into(target, *others):
    def one(i, carry):
        value = target[i]
        for other in others:
            value = value + other[i]
        target[i] = value
        return carry

    lax.fori_loop(0, target.shape[0], one, 0)


def march_kernel(
    steps,
    part, own, young, retarded, columns, inverse, out,
    gath, ret, quad, peer, zhalf, zfull, xhalf, xfull, yhalf, yfull,
    hsum, hhalf, hfull, base, new, newer, sols,
    send_sems, recv_sems, local_sems,
):
    panel, z = lax.axis_index("panel"), lax.axis_index("lag")
    c, x, y = panel % 2, (panel // 2) % RING, panel // (2 * RING)
    lags, own_blocks, knz, width, _ = ret.shape
    quarter = width // RING

    def hop(v, by):
        return lax.rem(v + (by + RING), RING)

    def at(yy, xx, cc):
        return (yy * RING + xx) * 2 + cc

    to_x = {d: (at(y, hop(x, d), c), z) for d in (1, -1)}
    to_y = {d: (at(hop(y, d), x, c), z) for d in (1, -1)}
    to_z = {d: (panel, hop(z, d)) for d in (1, -1)}
    to_mate = (at(y, x, 1 - c), z)

    used = [0]

    def copy(src, dst, to):
        i = used[0]
        used[0] += 1
        return pltpu.make_async_remote_copy(
            src_ref=src, dst_ref=dst, send_sem=send_sems.at[i], recv_sem=recv_sems.at[i],
            device_id=to, device_id_type=MESH,
        )

    started = []

    def go(*copies):
        for one in copies:
            one.start()
            started.append(one)

    def landed(*copies):
        for one in copies:
            one.wait_recv()

    class Gather:
        def __init__(self, view):
            whole = slice(None)
            self.first, self.pass_on, self.lines, self.line_on, self.mates = [], [], [], [], []
            for half, (near, wide) in enumerate(((to_x, to_y), (to_y, to_x))):

                def chunk(part, by, half=half):
                    return view(half, part, y, hop(x, by)) if half == 0 else view(half, part, hop(y, by), x)

                def line(part, by, half=half):
                    return view(half, part, hop(y, by), whole) if half == 0 else view(half, part, whole, hop(x, by))

                self.first.append([copy(chunk(None, 0), chunk(None, 0), near[d]) for d in (1, -1)])
                self.pass_on.append([
                    copy(chunk(0, -1), chunk(0, -1), near[1]),
                    copy(chunk(1, 1), chunk(1, 1), near[-1]),
                ])
                self.lines.append([copy(line(None, 0), line(None, 0), wide[d]) for d in (1, -1)])
                self.line_on.append([
                    copy(line(0, -1), line(0, -1), wide[1]),
                    copy(line(1, 1), line(1, 1), wide[-1]),
                ])
                self.mates.append([copy(line(None, by), line(None, by), to_mate) for by in (0, -1, 1, 2)])

        def all_copies(self):
            return [k for group in (self.first, self.pass_on, self.lines, self.line_on, self.mates) for h in group for k in h]

        def start(self, go):
            for half in (0, 1):
                go(*self.first[half])

        def pass_chunks(self, go):
            for half in (0, 1):
                for d in (0, 1):
                    landed(self.first[half][d])
                    go(self.pass_on[half][d])

        def send_lines(self, go):
            for half in (0, 1):
                landed(*self.pass_on[half])
                go(*self.lines[half], self.mates[half][0])

        def pass_lines(self, go):
            for half in (0, 1):
                for d in (0, 1):
                    landed(self.lines[half][d])
                    go(self.line_on[half][d], self.mates[half][1 + d])

        def last_lines(self, go):
            for half in (0, 1):
                landed(*self.line_on[half])
                go(self.mates[half][3])

        def finish(self):
            for half in (0, 1):
                landed(*self.mates[half])

    lead = RING - 2

    def past_view(half, part, yy, xx):
        first = lead * (1 - half)
        if part is None:
            return gath.at[pl.ds(first, 2), c, yy, xx]
        return gath.at[first + part, c, yy, xx]

    def new_view(buffer):
        def view(half, part, yy, xx):
            rows = width // 2
            first = half * rows
            if part is not None:
                rows = rows // 2
                first = first + part * rows
            return buffer.at[c, yy, xx, :, pl.ds(first, rows)]

        def lines(half, part, yy, xx):
            return view(half, part, yy, xx)

        return lines

    past = Gather(past_view)
    spread = [Gather(new_view(new)), Gather(new_view(newer))]

    class Ring:
        def __init__(self, me, to, chunk, part, half, full):
            up, down, far = hop(me, 1), hop(me, -1), hop(me, 2)
            self.mine = chunk(me)
            self.adds = [(part(up, 0), half(0)), (part(down, 1), half(1))]
            self.halves = [copy(part(far, 0), half(0), to[1]), copy(part(far, 1), half(1), to[-1])]
            self.fulls = [copy(chunk(up), full(0), to[1]), copy(chunk(down), full(1), to[-1])]
            self.arrived = [full(0), full(1)]

        def one(self):
            go(*self.halves)

        def two(self):
            for d in (0, 1):
                landed(self.halves[d])
                add_into(*self.adds[d])
                go(self.fulls[d])

        def three(self):
            landed(*self.fulls)

    cores = [copy(part.at[s, 1 - c], peer.at[s], to_mate) for s in range(steps)]
    kept = [pltpu.make_async_copy(part.at[s, c], quad.at[s], local_sems.at[s]) for s in range(steps)]
    matrices = pltpu.make_async_copy(retarded, ret, local_sems.at[steps])
    along_z, along_x, along_y = [], [], []
    for s in range(steps):
        along_z.append(Ring(
            z, to_z, lambda d, s=s: quad.at[s, d], lambda d, h, s=s: quad.at[s, d, pl.ds(2 * h, 2)],
            lambda i, s=s: zhalf.at[s, i], lambda i, s=s: zfull.at[s, i],
        ))
        along_x.append(Ring(
            x, to_x, lambda d, s=s: quad.at[s, z, :, d], lambda d, h, s=s: quad.at[s, z, pl.ds(2 * h, 2), d],
            lambda i, s=s: xhalf.at[s, i], lambda i, s=s: xfull.at[s, i],
        ))
        along_y.append(Ring(
            y, to_y, lambda d, s=s: quad.at[s, z, d, x],
            lambda d, h, s=s: quad.at[s, z, d, x, :, pl.ds(quarter // 2 * h, quarter // 2)],
            lambda i, s=s: yhalf.at[s, i], lambda i, s=s: yfull.at[s, i],
        ))
    older = Ring(
        z, to_z, lambda d: hsum.at[:, :, d], lambda d, h: hsum.at[:, :, d, pl.ds(quarter // 2 * h, quarter // 2)],
        lambda i: hhalf.at[i], lambda i: hfull.at[i],
    )

    right_first, right_on = [], []
    for s in range(steps):
        right_first.append([copy(base.at[s, :, z], base.at[s, :, z], to_z[d]) for d in (1, -1)])
        on = []
        for d, h in ((1, 0), (-1, 1)):
            piece = base.at[s, :, hop(z, -d), pl.ds(quarter // 2 * h, quarter // 2)]
            on.append(copy(piece, piece, to_z[d]))
        right_on.append(on)

    told = {s: [copy(sols.at[s], sols.at[s], to_z[d]) for d in (1, -1)] for s in range(1, steps)}
    told_on = {}
    for s in range(1, steps):
        pieces = [sols.at[s, :, pl.ds(h * (width // 2), width // 2)] for h in (0, 1)]
        told_on[s] = [copy(pieces[0], pieces[0], to_z[1]), copy(pieces[1], pieces[1], to_z[-1])]

    def field(buffer, lead_index, col):
        chip = col // (2 * own_blocks)
        where = ((col // own_blocks) % 2, chip // RING, chip % RING, col % own_blocks)
        return buffer[(*lead_index, *where)]

    def older_sums():
        def row(i, carry):
            lag, r = i // own_blocks, i % own_blocks
            total = jnp.zeros((width, steps * width), SUM)
            for k in range(0, knz, 2):
                left = jnp.concatenate([ret[lag, r, k], ret[lag, r, k + 1]], 1)
                fields = []
                for j in (k, k + 1):
                    col = columns[lag, r, j]
                    fields.append(jnp.concatenate([field(gath, (lag + steps - 1 - s,), col) for s in range(steps)], 1))
                total = total + jnp.dot(left, jnp.concatenate(fields, 0), preferred_element_type=SUM)
            for s in range(steps):
                value = total[:, s * width : (s + 1) * width].reshape(RING, quarter, width)
                hsum[s, r] += value
            return carry

        hsum[...] = jnp.zeros_like(hsum)
        lax.fori_loop(0, lags * own_blocks, row, 0)

    def newer_sum(s, r):
        total = jnp.zeros((width, width), SUM)
        for lag, buffer in ((0, new),) if s == 1 else ((0, newer), (1, new)):
            for k in range(0, knz, 2):
                left = jnp.concatenate([ret[lag, r, k], ret[lag, r, k + 1]], 1)
                fields = [field(buffer, (), columns[lag, r, j]) for j in (k, k + 1)]
                total = total + jnp.dot(left, jnp.concatenate(fields, 0), preferred_element_type=SUM)
        return total

    def solve(s):
        def row(r, carry):
            rhs = base[s, r].reshape(width, width)
            if s:
                rhs = rhs - newer_sum(s, r)
            value = jnp.dot(inverse[r], rhs, precision=lax.Precision.HIGHEST, preferred_element_type=SUM)
            sols[s, r] = value.astype(sols.dtype)
            return carry

        lax.fori_loop(0, own_blocks, row, 0)

    def to_base(s):
        landed(*along_y[s].fulls)
        quad_mine = quad[s, z, y, x] + yfull[s, 0] + yfull[s, 1]
        older_mine = hsum[s, :, z] + hfull[0, s] + hfull[1, s]
        base[s, :, z] = quad_mine - older_mine

    barrier = pltpu.get_barrier_semaphore()
    neighbours = [*to_x.values(), *to_y.values(), *to_z.values(), to_mate]
    for to in neighbours:
        pl.semaphore_signal(barrier, inc=1, device_id=to, device_id_type=MESH)
    pl.semaphore_wait(barrier, len(neighbours))

    for k in kept:
        k.start()
    matrices.start()
    go(cores[0])
    gath[pl.ds(lead, 2), c, y, x] = own[...]
    gath[pl.ds(0, 2), c, y, x] = young[...]
    past.start(go)
    go(*cores[1:])

    def over_cores(s):
        kept[s].wait()
        landed(cores[s])
        add_into(quad.at[s, hop(z, 2)], peer.at[s, hop(z, 2)])
        along_z[s].one()
        for by in (1, -1, 0):
            add_into(quad.at[s, hop(z, by)], peer.at[s, hop(z, by)])

    def z_to_x(s):
        along_z[s].three()
        add_into(along_z[s].mine, *along_z[s].arrived)
        along_x[s].one()

    def x_to_y(s):
        along_x[s].three()
        add_into(along_x[s].mine, *along_x[s].arrived)
        along_y[s].one()

    def right_side(s):
        to_base(s)
        go(*right_first[s])

    def right_pass(s):
        for d in (0, 1):
            landed(right_first[s][d])
            go(right_on[s][d])

    def right_done(s):
        landed(*right_on[s])

    def leading(act):
        pl.when(z == 0)(act)

    def only_start(*copies):
        for one in copies:
            one.start()

    over_cores(0)
    past.pass_chunks(go)
    past.send_lines(go)
    along_z[0].two()
    over_cores(1)
    past.pass_lines(go)
    z_to_x(0)
    along_z[1].two()
    over_cores(2)
    along_x[0].two()
    past.last_lines(go)
    x_to_y(0)
    past.finish()
    matrices.wait()
    older_sums()
    older.one()
    along_y[0].two()
    older.two()
    older.three()
    right_side(0)
    right_pass(0)
    right_done(0)
    solve(0)

    def send_first():
        new[c, y, x] = sols[0]
        spread[0].start(only_start)

    leading(send_first)
    z_to_x(1)
    along_z[2].two()
    leading(lambda: spread[0].pass_chunks(only_start))
    along_x[1].two()
    leading(lambda: spread[0].send_lines(only_start))
    x_to_y(1)
    along_y[1].two()
    leading(lambda: spread[0].pass_lines(only_start))
    right_side(1)
    right_pass(1)
    leading(lambda: spread[0].last_lines(only_start))
    right_done(1)

    def second():
        spread[0].finish()
        solve(1)
        newer[c, y, x] = sols[1]
        spread[1].start(only_start)
        only_start(*told[1])

    leading(second)
    z_to_x(2)
    leading(lambda: spread[1].pass_chunks(only_start))
    along_x[2].two()
    leading(lambda: spread[1].send_lines(only_start))
    x_to_y(2)
    along_y[2].two()
    leading(lambda: spread[1].pass_lines(only_start))
    right_side(2)
    right_pass(2)
    leading(lambda: spread[1].last_lines(only_start))
    right_done(2)

    def third():
        spread[1].finish()
        solve(2)
        only_start(*told[2])
        for gather in spread:
            for one in gather.all_copies():
                one.wait_send()
        for s in range(1, steps):
            for one in told[s]:
                one.wait_send()

    leading(third)

    for place, d in ((1, 0), (RING - 1, 1)):

        @pl.when(z == place)
        def pass_on(d=d):
            for s in range(1, steps):
                landed(told[s][d])
                told_on[s][d].start()
            for s in range(1, steps):
                told_on[s][d].wait_send()

    @pl.when(z == 2)
    def take():
        for s in range(1, steps):
            landed(*told_on[s])

    for one in started:
        one.wait_send()
    out[...] = sols[...]


def march(part, own, young, retarded, columns, inverse, steps):
    lags, own_blocks, knz, width, _ = retarded.shape
    quarter = width // RING
    cases = own.shape[-1]
    piece = (own_blocks, quarter, cases)
    halved = (own_blocks, quarter // 2, cases)
    bf16 = own.dtype
    plane = (2, RING, RING, own_blocks, width, cases)
    copies = 200
    return pl.pallas_call(
        functools.partial(march_kernel, steps),
        out_shape=jax.ShapeDtypeStruct((steps, own_blocks, width, cases), bf16),
        in_specs=[
            pl.BlockSpec(memory_space=pl.ANY),
            pl.BlockSpec(memory_space=pltpu.VMEM),
            pl.BlockSpec(memory_space=pltpu.VMEM),
            pl.BlockSpec(memory_space=pl.ANY),
            pl.BlockSpec(memory_space=pltpu.SMEM),
            pl.BlockSpec(memory_space=pltpu.VMEM),
        ],
        out_specs=pl.BlockSpec(memory_space=pltpu.VMEM),
        scratch_shapes=[
            pltpu.VMEM((RING, *plane), bf16),
            pltpu.VMEM(retarded.shape, bf16),
            pltpu.VMEM((steps, RING, RING, RING, *piece), SUM),
            pltpu.VMEM((steps, RING, RING, RING, *piece), SUM),
            pltpu.VMEM((steps, 2, RING // 2, RING, *piece), SUM),
            pltpu.VMEM((steps, 2, RING, RING, *piece), SUM),
            pltpu.VMEM((steps, 2, RING // 2, *piece), SUM),
            pltpu.VMEM((steps, 2, RING, *piece), SUM),
            pltpu.VMEM((steps, 2, *halved), SUM),
            pltpu.VMEM((steps, 2, *piece), SUM),
            pltpu.VMEM((steps, own_blocks, RING, quarter, cases), SUM),
            pltpu.VMEM((2, steps, *halved), SUM),
            pltpu.VMEM((2, steps, *piece), SUM),
            pltpu.VMEM((steps, own_blocks, RING, quarter, cases), SUM),
            pltpu.VMEM(plane, bf16),
            pltpu.VMEM(plane, bf16),
            pltpu.VMEM((steps, own_blocks, width, cases), bf16),
            pltpu.SemaphoreType.DMA((copies,)),
            pltpu.SemaphoreType.DMA((copies,)),
            pltpu.SemaphoreType.DMA((steps + 1,)),
        ],
        compiler_params=pltpu.CompilerParams(
            collective_id=0, has_side_effects=True, vmem_limit_bytes=60 * 2**20
        ),
    )(part, own, young, retarded, columns, inverse)


def local(strengths, incident_green, targets, history, retarded, columns, inverse):
    own_rows = history.shape[1]
    cases = history.shape[2]
    width = inverse.shape[1]
    own_blocks = inverse.shape[0]
    steps = strengths.shape[1] // cases
    younger = passed_along(history, "lag", 1)
    part = incident_partial(strengths, incident_green, targets, own_blocks, steps)
    part = part.reshape(steps, 2, RING, RING, RING, own_blocks, width // RING, cases)
    blocked = (history.shape[0], own_blocks, width, cases)
    solved = march(
        part, history.reshape(blocked), younger.reshape(blocked), retarded, columns, inverse, steps
    )
    return solved.reshape(steps, own_rows, cases)


def solution(mesh):
    placed = (
        P(("panel", "lag"), None),
        P(("panel", "lag"), None, None),
        P(("panel", "lag")),
        P("lag", "panel", None),
        P("lag", "panel", None, None, None),
        P("lag", "panel", None),
        P("panel", None, None),
    )
    return jax.shard_map(
        local, mesh=mesh, in_specs=placed, out_specs=P(None, "panel", None), check_vma=False
    )
```

```python
import functools

import jax
import jax.numpy as jnp
from jax import lax
from jax.experimental import pallas as pl
from jax.experimental.pallas import tpu as pltpu
from jax.sharding import PartitionSpec as P

MESH = pl.DeviceIdType.MESH
RING = 4
SUM = jnp.float32
CODE = jnp.int16
CODES = 32767.0
TINY = 1e-33


def incident_kernel(per_cell, steps, targets, green, cells, out, total, sem):
    group = pl.program_id(0)
    width = green.shape[1]
    own_blocks = total.shape[3]
    quarter = width // RING

    @pl.when(group == 0)
    def clear():
        def one(i, carry):
            total[i // (RING * RING), i % (RING * RING)] = jnp.zeros(total.shape[2:], SUM)
            return carry

        lax.fori_loop(0, steps * RING * RING, one, 0)

    def add_block(i, carry):
        target = targets[group * per_cell + i]
        device, block = target // own_blocks, target % own_blocks
        chip, core = device // 2, device % 2
        product = jnp.dot(green[i], cells[...], preferred_element_type=SUM)
        for s in range(steps):
            total[s, chip, core, block] += product[:, s * width : (s + 1) * width]
        return carry

    lax.fori_loop(0, per_cell, add_block, 0, unroll=4)

    @pl.when(group == pl.num_programs(0) - 1)
    def store():
        copies = []
        for s in range(steps):
            for core in range(2):
                for j in range(RING):
                    copies.append(
                        pltpu.make_async_copy(
                            total.at[s, :, core, :, pl.ds(j * quarter, quarter)],
                            out.at[s, core, j],
                            sem.at[s, core, j],
                        )
                    )
        for copy in copies:
            copy.start()
        for copy in copies:
            copy.wait()


def incident_partial(strengths, green, targets, own_blocks, steps):
    count, width, _ = green.shape
    cell_blocks = strengths.shape[0] // width
    per_cell = count // cell_blocks
    chips = RING * RING
    return pl.pallas_call(
        functools.partial(incident_kernel, per_cell, steps),
        out_shape=jax.ShapeDtypeStruct(
            (steps, 2, RING, chips, own_blocks, width // RING, width), SUM
        ),
        grid_spec=pltpu.PrefetchScalarGridSpec(
            num_scalar_prefetch=1,
            grid=(cell_blocks,),
            in_specs=[
                pl.BlockSpec((per_cell, width, width), lambda g, t: (g, 0, 0)),
                pl.BlockSpec((width, strengths.shape[1]), lambda g, t: (g, 0)),
            ],
            out_specs=pl.BlockSpec(memory_space=pl.ANY),
            scratch_shapes=[
                pltpu.VMEM((steps, chips, 2, own_blocks, width, width), SUM),
                pltpu.SemaphoreType.DMA((steps, 2, RING)),
            ],
        ),
        compiler_params=pltpu.CompilerParams(vmem_limit_bytes=60 * 2**20),
    )(targets, green, strengths)


def add_into(target, *others):
    def one(i, carry):
        value = target[i]
        for other in others:
            value = value + other[i]
        target[i] = value
        return carry

    lax.fori_loop(0, target.shape[0], one, 0)


def scales_of(value):
    top = jnp.max(jnp.abs(value), axis=-2, keepdims=True)
    tiny = top < TINY
    return jnp.where(tiny, 0.0, CODES / jnp.where(tiny, 1.0, top)), jnp.where(tiny, 0.0, top * (1.0 / CODES))


def encode(source, codes, scales):
    def one(i, carry):
        value = source[i]
        there, back = scales_of(value)
        codes[i] = jnp.round(value * there).astype(jnp.int32).astype(codes.dtype)
        scales[i] = jnp.squeeze(back, -2)
        return carry

    lax.fori_loop(0, source.shape[0], one, 0)


def decode(codes, scales, i):
    return codes[i].astype(jnp.int32).astype(SUM) * jnp.expand_dims(scales[i], -2)


def add_decoded(target, *arrived):
    def one(i, carry):
        value = target[i]
        for codes, scales in arrived:
            value = value + decode(codes, scales, i)
        target[i] = value
        return carry

    lax.fori_loop(0, target.shape[0], one, 0)


def march_kernel(
    steps,
    part, own, retarded, columns, inverse, out,
    gath, gath_young, ret, quad, peer, base, new, newer, sols, hsum, hgot, ygot,
    zhalf, zhalf_scale, zfull, zfull_scale, zhalf_out, zhalf_out_scale, zfull_out, zfull_out_scale,
    xgot, xgot_scale, xout, xout_scale,
    send_sems, recv_sems, local_sems,
):
    panel, z = lax.axis_index("panel"), lax.axis_index("lag")
    c, x, y = panel % 2, (panel // 2) % RING, panel // (2 * RING)
    lags, own_blocks, knz, width, _ = ret.shape
    quarter = width // RING
    others = (1, -1, 2)

    def hop(v, by):
        return lax.rem(v + (by + RING), RING)

    def at(yy, xx, cc):
        return (yy * RING + xx) * 2 + cc

    to_x = {d: (at(y, hop(x, d), c), z) for d in others}
    to_y = {d: (at(hop(y, d), x, c), z) for d in others}
    to_z = {d: (panel, hop(z, d)) for d in others}
    to_mate = (at(y, x, 1 - c), z)

    used = [0]

    def copy(src, dst, to):
        i = used[0]
        used[0] += 1
        return pltpu.make_async_remote_copy(
            src_ref=src, dst_ref=dst, send_sem=send_sems.at[i], recv_sem=recv_sems.at[i],
            device_id=to, device_id_type=MESH,
        )

    started = []

    def go(*copies):
        for one in copies:
            one.start()
            started.append(one)

    def only_start(*copies):
        for one in copies:
            one.start()

    def landed(*copies):
        for one in copies:
            one.wait_recv()

    class Gather:
        def __init__(self, view, go):
            whole = slice(None)
            self.go = go
            self.first, self.pass_on, self.lines, self.line_on, self.mates = [], [], [], [], []
            for half, (near, wide) in enumerate(((to_x, to_y), (to_y, to_x))):

                def chunk(part, by, half=half):
                    return view(half, part, y, hop(x, by)) if half == 0 else view(half, part, hop(y, by), x)

                def line(part, by, half=half):
                    return view(half, part, hop(y, by), whole) if half == 0 else view(half, part, whole, hop(x, by))

                def sent(what, part, by, to):
                    return copy(what(part, by), what(part, by), to)

                self.first.append([sent(chunk, None, 0, near[d]) for d in (1, -1)])
                self.pass_on.append([sent(chunk, 0, -1, near[1]), sent(chunk, 1, 1, near[-1])])
                self.lines.append([sent(line, None, 0, wide[d]) for d in (1, -1)])
                self.line_on.append([sent(line, 0, -1, wide[1]), sent(line, 1, 1, wide[-1])])
                self.mates.append([sent(line, None, by, to_mate) for by in (0, -1, 1, 2)])

        def all_copies(self):
            return [k for group in (self.first, self.pass_on, self.lines, self.line_on, self.mates) for h in group for k in h]

        def start(self):
            for half in (0, 1):
                self.go(*self.first[half])

        def pass_chunks(self):
            for d in (0, 1):
                for half in (0, 1):
                    landed(self.first[half][d])
                    self.go(self.pass_on[half][d])

        def send_lines(self):
            for half in (0, 1):
                landed(*self.pass_on[half])
                self.go(*self.lines[half])
            for half in (0, 1):
                self.go(self.mates[half][0])

        def pass_lines(self):
            for d in (0, 1):
                for half in (0, 1):
                    landed(self.lines[half][d])
                    self.go(self.line_on[half][d])
            for d in (0, 1):
                for half in (0, 1):
                    self.go(self.mates[half][1 + d])

        def last_lines(self):
            for half in (0, 1):
                landed(*self.line_on[half])
                self.go(self.mates[half][3])

        def finish(self):
            for half in (0, 1):
                landed(*self.mates[half])

        def wait_sends(self):
            for one in self.all_copies():
                one.wait_send()

    def halves_of(buffer, *front):
        def view(half, part, yy, xx):
            rows = width // 2
            first = half * rows
            if part is not None:
                rows = rows // 2
                first = first + part * rows
            return buffer.at[(*front, c, yy, xx, slice(None), pl.ds(first, rows))]

        return view

    past = Gather(halves_of(gath, slice(None)), go)
    young = Gather(halves_of(gath_young, slice(None)), only_start)
    spread = [Gather(halves_of(buffer), only_start) for buffer in (new, newer)]
    younger = copy(own, gath_young.at[:, c, y, x], to_z[1])

    cores = [copy(part.at[s, 1 - c], peer.at[s], to_mate) for s in range(steps)]
    kept = [pltpu.make_async_copy(part.at[s, c], quad.at[s], local_sems.at[s]) for s in range(steps)]
    matrices = pltpu.make_async_copy(retarded, ret, local_sems.at[steps])

    def both(codes, scales, got, got_scales, to):
        return [copy(codes, got, to), copy(scales, got_scales, to)]

    z_halves, z_fulls, x_all, y_all = [], [], [], []
    for s in range(steps):
        z_halves.append([
            both(zhalf_out.at[s, i], zhalf_out_scale.at[s, i], zhalf.at[s, i], zhalf_scale.at[s, i], to_z[d])
            for i, d in enumerate((1, -1))
        ])
        z_fulls.append([
            both(zfull_out.at[s, i], zfull_out_scale.at[s, i], zfull.at[s, i], zfull_scale.at[s, i], to_z[d])
            for i, d in enumerate((1, -1))
        ])
        x_all.append([
            both(xout.at[s, i], xout_scale.at[s, i], xgot.at[s, i], xgot_scale.at[s, i], to_x[d])
            for i, d in enumerate(others)
        ])
        y_all.append([copy(quad.at[s, z, hop(y, d), x], ygot.at[s, i], to_y[d]) for i, d in enumerate(others)])

    def over_cores(s):
        kept[s].wait()
        landed(cores[s])
        far = hop(z, 2)
        add_into(quad.at[s, far], peer.at[s, far])
        for i in (0, 1):
            encode(quad.at[s, far, pl.ds(2 * i, 2)], zhalf_out.at[s, i], zhalf_out_scale.at[s, i])
            go(*z_halves[s][i])
        for by in (1, -1, 0):
            add_into(quad.at[s, hop(z, by)], peer.at[s, hop(z, by)])

    def z_pass(s):
        for i, d in enumerate((1, -1)):
            landed(*z_halves[s][i])
            there = hop(z, d)
            add_decoded(quad.at[s, there, pl.ds(2 * i, 2)], (zhalf.at[s, i], zhalf_scale.at[s, i]))
            encode(quad.at[s, there], zfull_out.at[s, i], zfull_out_scale.at[s, i])
            go(*z_fulls[s][i])

    def z_to_x(s):
        for i in (0, 1):
            landed(*z_fulls[s][i])
        add_decoded(quad.at[s, z], *((zfull.at[s, i], zfull_scale.at[s, i]) for i in (0, 1)))
        for i, d in enumerate(others):
            encode(quad.at[s, z, :, hop(x, d)], xout.at[s, i], xout_scale.at[s, i])
            go(*x_all[s][i])

    def x_to_y(s):
        for one in x_all[s]:
            landed(*one)
        add_decoded(quad.at[s, z, :, x], *((xgot.at[s, i], xgot_scale.at[s, i]) for i in range(3)))
        go(*y_all[s])

    groups = ((0, 1), (1, steps - 1))
    older = [
        [
            copy(hsum.at[pl.ds(first, n), :, hop(z, d)], hgot.at[i, pl.ds(first, n)], to_z[d])
            for i, d in enumerate(others)
        ]
        for first, n in groups
    ]
    right = [[copy(base.at[s, :, z], base.at[s, :, z], to_z[d]) for d in others] for s in range(steps)]

    def right_side(s):
        landed(*y_all[s])
        total = quad[s, z, y, x] - hsum[s, :, z]
        for i in range(3):
            total = total + (ygot[s, i] - hgot[i, s])
        base[s, :, z] = total
        go(*right[s])

    told = {s: [copy(sols.at[s], sols.at[s], to_z[d]) for d in (1, -1)] for s in range(1, steps)}
    told_on = {}
    for s in range(1, steps):
        pieces = [sols.at[s, :, pl.ds(h * (width // 2), width // 2)] for h in (0, 1)]
        told_on[s] = [copy(pieces[0], pieces[0], to_z[1]), copy(pieces[1], pieces[1], to_z[-1])]

    def field(buffer, front, col):
        chip = col // (2 * own_blocks)
        where = ((col // own_blocks) % 2, chip // RING, chip % RING, col % own_blocks)
        return buffer[(*front, *where)]

    def pairs(lag, r, fields):
        total = None
        for k in range(0, knz, 2):
            left = jnp.concatenate([ret[lag, r, k], ret[lag, r, k + 1]], 1)
            low = jnp.concatenate([fields(columns[lag, r, k]), fields(columns[lag, r, k + 1])], 0)
            product = jnp.dot(left, low, preferred_element_type=SUM)
            total = product if total is None else total + product
        return total

    def older_sums(first, n):
        def row(r, carry):
            total = None
            for lag in range(lags):

                def fields(col, lag=lag):
                    entries = [lag - s for s in range(first, first + n)]
                    found = [field(gath, (e,), col) if e >= 0 else field(gath_young, (lags + e,), col) for e in entries]
                    return jnp.concatenate(found, 1)

                value = pairs(lag, r, fields)
                total = value if total is None else total + value
            for j in range(n):
                hsum[first + j, r] = total[:, j * width : (j + 1) * width].reshape(RING, quarter, width)
            return carry

        lax.fori_loop(0, own_blocks, row, 0)

    def solve(s):
        def row(r, carry):
            rhs = base[s, r].reshape(width, width)
            if s:
                for lag, buffer in ((0, new),) if s == 1 else ((1, new), (0, newer)):
                    rhs = rhs - pairs(lag, r, lambda col, buffer=buffer: field(buffer, (), col))
            value = jnp.dot(inverse[r], rhs, precision=lax.Precision.HIGHEST, preferred_element_type=SUM)
            sols[s, r] = value.astype(sols.dtype)
            return carry

        lax.fori_loop(0, own_blocks, row, 0)

    def leading(act):
        pl.when(z == 0)(act)

    def following(act):
        pl.when(z > 0)(act)

    barrier = pltpu.get_barrier_semaphore()
    neighbours = [*to_x.values(), *to_y.values(), *to_z.values(), to_mate]
    for to in neighbours:
        pl.semaphore_signal(barrier, inc=1, device_id=to, device_id_type=MESH)
    for k in kept:
        k.start()
    matrices.start()
    gath[:, c, y, x] = own[...]
    pl.semaphore_wait(barrier, len(neighbours))

    go(cores[0])
    past.start()
    pl.when(z < RING - 1)(younger.start)
    go(*cores[1:])

    def nothing_younger():
        def clear(i, carry):
            gath_young[i // (2 * RING), (i // RING) % 2, i % RING] = jnp.zeros(gath_young.shape[3:], gath_young.dtype)
            return carry

        lax.fori_loop(0, 4 * RING, clear, 0)

    leading(nothing_younger)

    def start_young():
        landed(younger)
        young.start()

    over_cores(0)
    past.pass_chunks()
    past.send_lines()
    following(start_young)
    z_pass(0)
    over_cores(1)
    following(young.pass_chunks)
    past.pass_lines()
    following(young.send_lines)
    z_to_x(0)
    z_pass(1)
    over_cores(2)
    past.last_lines()
    x_to_y(0)
    matrices.wait()
    past.finish()
    older_sums(*groups[0])
    go(*older[0])
    z_pass(2)
    landed(*older[0])
    right_side(0)
    following(young.pass_lines)
    landed(*right[0])
    solve(0)

    def send_first():
        new[c, y, x] = sols[0]
        spread[0].start()

    leading(send_first)
    z_to_x(1)
    following(young.last_lines)
    leading(spread[0].pass_chunks)
    x_to_y(1)
    leading(spread[0].send_lines)
    following(young.finish)
    older_sums(*groups[1])
    go(*older[1])
    z_to_x(2)
    leading(spread[0].pass_lines)
    x_to_y(2)
    landed(*older[1])
    right_side(1)
    right_side(2)
    landed(*right[1])

    def second():
        spread[0].last_lines()
        spread[0].finish()
        solve(1)
        newer[c, y, x] = sols[1]
        spread[1].start()
        only_start(*told[1])

    leading(second)
    landed(*right[2])

    def third():
        spread[1].pass_chunks()
        spread[1].send_lines()
        spread[1].pass_lines()
        spread[1].last_lines()
        spread[1].finish()
        solve(2)
        only_start(*told[2])
        for gather in spread:
            gather.wait_sends()
        for s in range(1, steps):
            for one in told[s]:
                one.wait_send()

    leading(third)

    for place, d in ((1, 0), (RING - 1, 1)):

        @pl.when(z == place)
        def pass_on(d=d):
            for s in range(1, steps):
                landed(told[s][d])
                told_on[s][d].start()
            for s in range(1, steps):
                told_on[s][d].wait_send()

    @pl.when(z == 2)
    def take():
        for s in range(1, steps):
            landed(*told_on[s])

    pl.when(z < RING - 1)(younger.wait_send)
    following(young.wait_sends)
    for one in started:
        one.wait_send()
    out[...] = sols[...]


def march(part, own, retarded, columns, inverse, steps):
    lags, own_blocks, knz, width, _ = retarded.shape
    quarter = width // RING
    cases = own.shape[-1]
    piece = (own_blocks, quarter, cases)
    line = (own_blocks, cases)
    bf16 = own.dtype
    plane = (2, RING, RING, own_blocks, width, cases)
    halves, fulls, direct = (steps, 2, RING // 2, RING), (steps, 2, RING, RING), (steps, 3, RING)

    def coded(lead):
        return [pltpu.VMEM((*lead, *piece), CODE), pltpu.VMEM((*lead, *line), SUM)]

    copies = 240
    return pl.pallas_call(
        functools.partial(march_kernel, steps),
        out_shape=jax.ShapeDtypeStruct((steps, own_blocks, width, cases), bf16),
        in_specs=[
            pl.BlockSpec(memory_space=pl.ANY),
            pl.BlockSpec(memory_space=pltpu.VMEM),
            pl.BlockSpec(memory_space=pl.ANY),
            pl.BlockSpec(memory_space=pltpu.SMEM),
            pl.BlockSpec(memory_space=pltpu.VMEM),
        ],
        out_specs=pl.BlockSpec(memory_space=pltpu.VMEM),
        scratch_shapes=[
            pltpu.VMEM((lags, *plane), bf16),
            pltpu.VMEM((lags, *plane), bf16),
            pltpu.VMEM(retarded.shape, bf16),
            pltpu.VMEM((steps, RING, RING, RING, *piece), SUM),
            pltpu.VMEM((steps, RING, RING, RING, *piece), SUM),
            pltpu.VMEM((steps, own_blocks, RING, quarter, cases), SUM),
            pltpu.VMEM(plane, bf16),
            pltpu.VMEM(plane, bf16),
            pltpu.VMEM((steps, own_blocks, width, cases), bf16),
            pltpu.VMEM((steps, own_blocks, RING, quarter, cases), SUM),
            pltpu.VMEM((3, steps, *piece), SUM),
            pltpu.VMEM((steps, 3, *piece), SUM),
            *coded(halves), *coded(fulls), *coded(halves), *coded(fulls),
            *coded(direct), *coded(direct),
            pltpu.SemaphoreType.DMA((copies,)),
            pltpu.SemaphoreType.DMA((copies,)),
            pltpu.SemaphoreType.DMA((steps + 1,)),
        ],
        compiler_params=pltpu.CompilerParams(
            collective_id=0, has_side_effects=True, vmem_limit_bytes=60 * 2**20
        ),
    )(part, own, retarded, columns, inverse)


def local(strengths, incident_green, targets, history, retarded, columns, inverse):
    own_rows = history.shape[1]
    cases = history.shape[2]
    width = inverse.shape[1]
    own_blocks = inverse.shape[0]
    steps = strengths.shape[1] // cases
    part = incident_partial(strengths, incident_green, targets, own_blocks, steps)
    part = part.reshape(steps, 2, RING, RING, RING, own_blocks, width // RING, cases)
    blocked = (history.shape[0], own_blocks, width, cases)
    solved = march(part, history.reshape(blocked), retarded, columns, inverse, steps)
    return solved.reshape(steps, own_rows, cases)


def solution(mesh):
    placed = (
        P(("panel", "lag"), None),
        P(("panel", "lag"), None, None),
        P(("panel", "lag")),
        P("lag", "panel", None),
        P("lag", "panel", None, None, None),
        P("lag", "panel", None),
        P("panel", None, None),
    )
    return jax.shard_map(
        local, mesh=mesh, in_specs=placed, out_specs=P(None, "panel", None), check_vma=False
    )
```

```python
import functools

import jax
import jax.numpy as jnp
from jax import lax
from jax.experimental import pallas as pl
from jax.experimental.pallas import tpu as pltpu
from jax.sharding import PartitionSpec as P

MESH = pl.DeviceIdType.MESH
RING = 4
SUM = jnp.float32
CODE = jnp.int16
CODES = 32767.0
TINY = 1e-33


def incident_kernel(per_cell, steps, targets, green, cells, out, total, sem):
    group = pl.program_id(0)
    width = green.shape[1]
    own_blocks = total.shape[3]
    quarter = width // RING

    @pl.when(group == 0)
    def clear():
        def one(i, carry):
            total[i // (RING * RING), i % (RING * RING)] = jnp.zeros(total.shape[2:], SUM)
            return carry

        lax.fori_loop(0, steps * RING * RING, one, 0)

    def add_block(i, carry):
        target = targets[group * per_cell + i]
        device, block = target // own_blocks, target % own_blocks
        chip, core = device // 2, device % 2
        product = jnp.dot(green[i], cells[...], preferred_element_type=SUM)
        for s in range(steps):
            total[s, chip, core, block] += product[:, s * width : (s + 1) * width]
        return carry

    lax.fori_loop(0, per_cell, add_block, 0, unroll=4)

    @pl.when(group == pl.num_programs(0) - 1)
    def store():
        copies = []
        for s in range(steps):
            for core in range(2):
                for j in range(RING):
                    copies.append(
                        pltpu.make_async_copy(
                            total.at[s, :, core, :, pl.ds(j * quarter, quarter)],
                            out.at[s, core, j],
                            sem.at[s, core, j],
                        )
                    )
        for copy in copies:
            copy.start()
        for copy in copies:
            copy.wait()


def incident_partial(strengths, green, targets, own_blocks, steps):
    count, width, _ = green.shape
    cell_blocks = strengths.shape[0] // width
    per_cell = count // cell_blocks
    chips = RING * RING
    return pl.pallas_call(
        functools.partial(incident_kernel, per_cell, steps),
        out_shape=jax.ShapeDtypeStruct(
            (steps, 2, RING, chips, own_blocks, width // RING, width), SUM
        ),
        grid_spec=pltpu.PrefetchScalarGridSpec(
            num_scalar_prefetch=1,
            grid=(cell_blocks,),
            in_specs=[
                pl.BlockSpec((per_cell, width, width), lambda g, t: (g, 0, 0)),
                pl.BlockSpec((width, strengths.shape[1]), lambda g, t: (g, 0)),
            ],
            out_specs=pl.BlockSpec(memory_space=pl.ANY),
            scratch_shapes=[
                pltpu.VMEM((steps, chips, 2, own_blocks, width, width), SUM),
                pltpu.SemaphoreType.DMA((steps, 2, RING)),
            ],
        ),
        compiler_params=pltpu.CompilerParams(vmem_limit_bytes=60 * 2**20),
    )(targets, green, strengths)


def add_into(target, *others):
    def one(i, carry):
        value = target[i]
        for other in others:
            value = value + other[i]
        target[i] = value
        return carry

    lax.fori_loop(0, target.shape[0], one, 0)


def scales_of(value):
    top = jnp.max(jnp.abs(value), axis=-2, keepdims=True)
    tiny = top < TINY
    return jnp.where(tiny, 0.0, CODES / jnp.where(tiny, 1.0, top)), jnp.where(tiny, 0.0, top * (1.0 / CODES))


def encode(source, codes, scales):
    def one(i, carry):
        value = source[i]
        there, back = scales_of(value)
        codes[i] = jnp.round(value * there).astype(jnp.int32).astype(codes.dtype)
        scales[i] = jnp.squeeze(back, -2)
        return carry

    lax.fori_loop(0, source.shape[0], one, 0)


def decode(codes, scales, i):
    return codes[i].astype(jnp.int32).astype(SUM) * jnp.expand_dims(scales[i], -2)


def add_decoded(target, *arrived):
    def one(i, carry):
        value = target[i]
        for codes, scales in arrived:
            value = value + decode(codes, scales, i)
        target[i] = value
        return carry

    lax.fori_loop(0, target.shape[0], one, 0)


def march_kernel(
    steps,
    part, own, retarded, columns, inverse, out,
    gath, gath_young, ret, quad, peer, base, new, newer, sols, hsum, hgot, ygot,
    zhalf, zhalf_scale, zfull, zfull_scale, zhalf_out, zhalf_out_scale, zfull_out, zfull_out_scale,
    xgot, xgot_scale, xout, xout_scale,
    send_sems, recv_sems, local_sems,
):
    panel, z = lax.axis_index("panel"), lax.axis_index("lag")
    c, x, y = panel % 2, (panel // 2) % RING, panel // (2 * RING)
    lags, own_blocks, knz, width, _ = ret.shape
    quarter = width // RING
    others = (1, -1, 2)

    def hop(v, by):
        return lax.rem(v + (by + RING), RING)

    def at(yy, xx, cc):
        return (yy * RING + xx) * 2 + cc

    to_x = {d: (at(y, hop(x, d), c), z) for d in others}
    to_y = {d: (at(hop(y, d), x, c), z) for d in others}
    to_z = {d: (panel, hop(z, d)) for d in others}
    to_mate = (at(y, x, 1 - c), z)

    used = [0]

    def copy(src, dst, to):
        i = used[0]
        used[0] += 1
        return pltpu.make_async_remote_copy(
            src_ref=src, dst_ref=dst, send_sem=send_sems.at[i], recv_sem=recv_sems.at[i],
            device_id=to, device_id_type=MESH,
        )

    started = []

    def go(*copies):
        for one in copies:
            one.start()
            if not any(one is known for known in started):
                started.append(one)

    def only_start(*copies):
        for one in copies:
            one.start()

    def drain(n):
        for one in started[:n]:
            one.wait_send()
        del started[:n]

    def landed(*copies):
        for one in copies:
            one.wait_recv()

    class Gather:
        def __init__(self, view, go):
            whole = slice(None)
            self.go = go
            self.first, self.pass_on, self.wide, self.wide_on, self.mates = [], [], [], [], []
            for half, (near, far) in enumerate(((to_x, to_y), (to_y, to_x))):

                def spot(part, by, wide_by, half=half):
                    if half == 0:
                        return view(half, part, hop(y, wide_by), hop(x, by))
                    return view(half, part, hop(y, by), hop(x, wide_by))

                def line(wide_by, half=half):
                    return view(half, None, hop(y, wide_by), whole) if half == 0 else view(half, None, whole, hop(x, wide_by))

                def sent(part, by, wide_by, to):
                    return copy(spot(part, by, wide_by), spot(part, by, wide_by), to)

                self.first.append([sent(None, 0, 0, near[d]) for d in (1, -1)])
                self.pass_on.append([sent(0, -1, 0, near[1]), sent(1, 1, 0, near[-1])])
                self.wide.append({by: [sent(None, by, 0, far[d]) for d in (1, -1)] for by in (0, -1, 1, 2)})
                self.wide_on.append({by: [sent(0, by, -1, far[1]), sent(1, by, 1, far[-1])] for by in (0, -1, 1, 2)})
                self.mates.append([copy(line(by), line(by), to_mate) for by in (0, -1, 1, 2)])

        def start(self):
            for half in (0, 1):
                self.go(*self.first[half])
            for half in (0, 1):
                self.go(*self.wide[half][0])

        def pass_chunks(self):
            for d, by in ((0, -1), (1, 1)):
                for half in (0, 1):
                    landed(self.first[half][d])
                    self.go(self.pass_on[half][d])
            for by in (-1, 1):
                for half in (0, 1):
                    self.go(*self.wide[half][by])

        def far_chunk(self):
            for half in (0, 1):
                landed(*self.pass_on[half])
                self.go(*self.wide[half][2])
            for half in (0, 1):
                self.go(self.mates[half][0])

        def pass_wide(self, *which):
            for by in which:
                for d in (0, 1):
                    for half in (0, 1):
                        landed(self.wide[half][by][d])
                        self.go(self.wide_on[half][by][d])

        def pass_own(self):
            self.pass_wide(0)

        def pass_near(self):
            self.pass_wide(-1, 1)

        def pass_far(self):
            self.pass_wide(2)
            for d in (0, 1):
                for half in (0, 1):
                    self.go(self.mates[half][1 + d])

        def finish(self):
            for half in (0, 1):
                for by in (0, -1, 1, 2):
                    landed(*self.wide_on[half][by])
                self.go(self.mates[half][3])
            for half in (0, 1):
                landed(*self.mates[half])

        def wait_sends(self):
            for half in (0, 1):
                for group in (self.first, self.pass_on, self.mates, self.wide, self.wide_on):
                    members = group[half]
                    if isinstance(members, dict):
                        members = [one for pair in members.values() for one in pair]
                    for one in members:
                        one.wait_send()

    def halves_of(buffer, *front):
        def view(half, part, yy, xx):
            rows = width // 2
            first = half * rows
            if part is not None:
                rows = rows // 2
                first = first + part * rows
            return buffer.at[(*front, c, yy, xx, slice(None), pl.ds(first, rows))]

        return view

    past = Gather(halves_of(gath, slice(None)), go)
    between = used[0]
    young = Gather(halves_of(gath_young, slice(None)), only_start)
    used[0] = between
    spread = [Gather(halves_of(new), only_start)]
    used[0] = 0
    spread.append(Gather(halves_of(newer), only_start))
    used[0] = 2 * between
    younger = copy(own, gath_young.at[:, c, y, x], to_z[1])

    place, towards = {"z": z, "y": y, "x": x}, {"z": to_z, "y": to_y, "x": to_x}
    orders = ["zxy"] * (steps - 1) + ["xyz"]
    ordered = (2, 1, -1, 0)
    whole = slice(None)

    def cut(array, *front, **where):
        return array.at[(*front, *(where.get(axis, whole) for axis in "zyx"))]

    cores, kept = [], []
    for s, (a, _, _) in enumerate(orders):
        chunks = [{a: hop(place[a], by)} for by in ordered]
        cores.append([copy(cut(part, s, 1 - c, **at_chunk), cut(peer, s, **at_chunk), to_mate) for at_chunk in chunks])
        kept.append([
            pltpu.make_async_copy(cut(part, s, c, **at_chunk), cut(quad, s, **at_chunk), local_sems.at[s, i])
            for i, at_chunk in enumerate(chunks)
        ])
    matrices = pltpu.make_async_copy(retarded, ret, local_sems.at[steps, 0])

    def both(codes, scales, got, got_scales, to):
        return [copy(codes, got, to), copy(scales, got_scales, to)]

    ring_far, ring_free, ring_tied, second_all, third_all = [], [], [], [], []
    for s, (first, then, last) in enumerate(orders):
        to = towards[first]
        ring_far.append([
            both(zhalf_out.at[s, i], zhalf_out_scale.at[s, i], zhalf.at[s, i], zhalf_scale.at[s, i], to[d])
            for i, d in enumerate((1, -1))
        ])

        def near_half(i, h, s=s, to=to):
            rows = pl.ds(2 * h, 2)
            return both(
                zfull_out.at[s, i, rows], zfull_out_scale.at[s, i, rows], zfull.at[s, i, rows],
                zfull_scale.at[s, i, rows], to[(1, -1)[i]],
            )

        ring_free.append([near_half(i, 1 - i) for i in (0, 1)])
        ring_tied.append([near_half(i, i) for i in (0, 1)])
        second_all.append([
            both(xout.at[s, i], xout_scale.at[s, i], xgot.at[s, i], xgot_scale.at[s, i], towards[then][d])
            for i, d in enumerate(others)
        ])
        third_all.append([
            copy(
                cut(quad, s, **{first: place[first], then: place[then], last: hop(place[last], d)}),
                ygot.at[s, i], towards[last][d],
            )
            for i, d in enumerate(others)
        ])

    def ring_part(s, by, h=None):
        first, _, last = orders[s]
        where = {first: hop(place[first], by)}
        if h is not None:
            where[last] = pl.ds(2 * h, 2)
        return cut(quad, s, **where)

    def send_near(s, i, h, copies):
        rows = pl.ds(2 * h, 2)
        encode(ring_part(s, (1, -1)[i], h), zfull_out.at[s, i, rows], zfull_out_scale.at[s, i, rows])
        go(*copies)

    def over_cores(s):
        first = orders[s][0]
        for j, by in enumerate(ordered):
            kept[s][j].wait()
            landed(cores[s][j])
            add_into(ring_part(s, by), cut(peer, s, **{first: hop(place[first], by)}))
            if by == 2:
                for i in (0, 1):
                    encode(ring_part(s, by, i), zhalf_out.at[s, i], zhalf_out_scale.at[s, i])
                    go(*ring_far[s][i])
            elif by:
                i = (1, -1).index(by)
                send_near(s, i, 1 - i, ring_free[s][i])

    def ring_pass(s):
        for i, d in enumerate((1, -1)):
            landed(*ring_far[s][i])
            add_decoded(ring_part(s, d, i), (zhalf.at[s, i], zhalf_scale.at[s, i]))
            send_near(s, i, i, ring_tied[s][i])

    def to_second(s):
        first, then, _ = orders[s]
        for i in (0, 1):
            landed(*ring_free[s][i], *ring_tied[s][i])
        add_decoded(ring_part(s, 0), *((zfull.at[s, i], zfull_scale.at[s, i]) for i in (0, 1)))
        for i, d in enumerate(others):
            encode(cut(quad, s, **{first: place[first], then: hop(place[then], d)}), xout.at[s, i], xout_scale.at[s, i])
            go(*second_all[s][i])

    def to_third(s):
        first, then, _ = orders[s]
        for one in second_all[s]:
            landed(*one)
        mine = cut(quad, s, **{first: place[first], then: place[then]})
        add_decoded(mine, *((xgot.at[s, i], xgot_scale.at[s, i]) for i in range(3)))
        go(*third_all[s])

    groups = [(s, 1) for s in range(steps)]
    older = [
        [
            copy(hsum.at[pl.ds(first, n), :, hop(z, d)], hgot.at[i, pl.ds(first, n)], to_z[d])
            for i, d in enumerate(others)
        ]
        for first, n in groups
    ]
    right = [[copy(base.at[s, :, z], base.at[s, :, z], to_z[d]) for d in others] for s in range(steps)]

    def right_side(s):
        landed(*third_all[s])
        total = quad[s, z, y, x] - hsum[s, :, z]
        for i in range(3):
            total = total + (ygot[s, i] - hgot[i, s])
        base[s, :, z] = total
        go(*right[s])

    told = {s: [copy(sols.at[s], sols.at[s], to_z[d]) for d in others] for s in range(1, steps)}

    def field(buffer, front, col):
        chip = col // (2 * own_blocks)
        where = ((col // own_blocks) % 2, chip // RING, chip % RING, col % own_blocks)
        return buffer[(*front, *where)]

    def pairs(lag, r, fields):
        total = None
        for k in range(0, knz, 2):
            left = jnp.concatenate([ret[lag, r, k], ret[lag, r, k + 1]], 1)
            low = jnp.concatenate([fields(columns[lag, r, k]), fields(columns[lag, r, k + 1])], 0)
            product = jnp.dot(left, low, preferred_element_type=SUM)
            total = product if total is None else total + product
        return total

    def older_sums(first, n):
        def row(r, carry):
            total = None
            for lag in range(lags):

                def fields(col, lag=lag):
                    entries = [lag - s for s in range(first, first + n)]
                    found = [field(gath, (e,), col) if e >= 0 else field(gath_young, (lags + e,), col) for e in entries]
                    return jnp.concatenate(found, 1)

                value = pairs(lag, r, fields)
                total = value if total is None else total + value
            for j in range(n):
                hsum[first + j, r] = total[:, j * width : (j + 1) * width].reshape(RING, quarter, width)
            return carry

        lax.fori_loop(0, own_blocks, row, 0)

    def solve(s):
        def row(r, carry):
            rhs = base[s, r].reshape(width, width)
            if s:
                for lag, buffer in ((0, new),) if s == 1 else ((1, new), (0, newer)):
                    rhs = rhs - pairs(lag, r, lambda col, buffer=buffer: field(buffer, (), col))
            value = jnp.dot(inverse[r], rhs, precision=lax.Precision.HIGHEST, preferred_element_type=SUM)
            sols[s, r] = value.astype(sols.dtype)
            return carry

        lax.fori_loop(0, own_blocks, row, 0)

    def leading(act):
        pl.when(z == 0)(act)

    def following(act):
        pl.when(z > 0)(act)

    barrier = pltpu.get_barrier_semaphore()
    neighbours = [*to_x.values(), *to_y.values(), *to_z.values(), to_mate]
    for to in neighbours:
        pl.semaphore_signal(barrier, inc=1, device_id=to, device_id_type=MESH)
    for pieces in kept:
        for k in pieces:
            k.start()
    matrices.start()
    gath[:, c, y, x] = own[...]
    pl.semaphore_wait(barrier, len(neighbours))

    go(*cores[0])
    past.start()
    pl.when(z < RING - 1)(younger.start)
    for pieces in cores[1:]:
        go(*pieces)

    def nothing_younger():
        def clear(i, carry):
            gath_young[i // (2 * RING), (i // RING) % 2, i % RING] = jnp.zeros(gath_young.shape[3:], gath_young.dtype)
            return carry

        lax.fori_loop(0, 4 * RING, clear, 0)

    leading(nothing_younger)

    def start_young():
        landed(younger)
        young.start()

    over_cores(0)
    past.pass_chunks()
    past.far_chunk()
    ring_pass(0)
    past.pass_own()
    over_cores(1)
    past.pass_near()
    past.pass_far()
    following(start_young)
    to_second(0)
    matrices.wait()
    past.finish()
    leading(lambda: over_cores(2))
    older_sums(*groups[0])
    go(*older[0])
    following(young.pass_chunks)
    to_third(0)
    following(young.far_chunk)
    landed(*older[0])
    right_side(0)
    ring_pass(1)
    following(young.pass_own)
    following(young.pass_near)
    leading(lambda: ring_pass(2))
    following(young.pass_far)
    landed(*right[0])
    solve(0)

    def send_first():
        new[c, y, x] = sols[0]
        spread[0].start()

    leading(send_first)
    following(lambda: over_cores(2))
    to_second(1)
    following(young.finish)
    older_sums(*groups[1])
    go(*older[1])
    leading(spread[0].pass_chunks)
    following(lambda: ring_pass(2))
    leading(spread[0].far_chunk)
    to_third(1)
    landed(*older[1])
    leading(spread[0].pass_own)
    leading(spread[0].pass_near)
    old = len(started)
    right_side(1)
    older_sums(*groups[2])
    go(*older[2])
    leading(spread[0].pass_far)
    to_second(2)
    drain(old)
    landed(*right[1])

    def second():
        spread[0].finish()
        solve(1)
        newer[c, y, x] = sols[1]
        spread[1].start()
        only_start(*told[1])

    leading(second)
    to_third(2)
    leading(spread[1].pass_chunks)
    landed(*older[2])
    leading(spread[1].far_chunk)
    right_side(2)
    leading(spread[0].wait_sends)
    leading(spread[1].pass_own)
    leading(spread[1].pass_near)
    leading(spread[1].pass_far)
    landed(*right[2])

    def third():
        spread[1].finish()
        solve(2)
        only_start(*told[2])
        spread[1].wait_sends()
        for s in range(1, steps):
            for one in told[s]:
                one.wait_send()

    leading(third)

    for i, d in enumerate(others):

        @pl.when(z == d % RING)
        def take(i=i):
            for s in range(1, steps):
                landed(told[s][i])

    pl.when(z < RING - 1)(younger.wait_send)
    following(young.wait_sends)
    for one in started:
        one.wait_send()
    out[...] = sols[...]
    assert used[0] <= send_sems.shape[0], used[0]


def march(part, own, retarded, columns, inverse, steps):
    lags, own_blocks, knz, width, _ = retarded.shape
    quarter = width // RING
    cases = own.shape[-1]
    piece = (own_blocks, quarter, cases)
    line = (own_blocks, cases)
    bf16 = own.dtype
    plane = (2, RING, RING, own_blocks, width, cases)
    halves, fulls, direct = (steps, 2, RING // 2, RING), (steps, 2, RING, RING), (steps, 3, RING)

    def coded(lead):
        return [pltpu.VMEM((*lead, *piece), CODE), pltpu.VMEM((*lead, *line), SUM)]

    copies = 196
    return pl.pallas_call(
        functools.partial(march_kernel, steps),
        out_shape=jax.ShapeDtypeStruct((steps, own_blocks, width, cases), bf16),
        in_specs=[
            pl.BlockSpec(memory_space=pl.ANY),
            pl.BlockSpec(memory_space=pltpu.VMEM),
            pl.BlockSpec(memory_space=pl.ANY),
            pl.BlockSpec(memory_space=pltpu.SMEM),
            pl.BlockSpec(memory_space=pltpu.VMEM),
        ],
        out_specs=pl.BlockSpec(memory_space=pltpu.VMEM),
        scratch_shapes=[
            pltpu.VMEM((lags, *plane), bf16),
            pltpu.VMEM((lags, *plane), bf16),
            pltpu.VMEM(retarded.shape, bf16),
            pltpu.VMEM((steps, RING, RING, RING, *piece), SUM),
            pltpu.VMEM((steps, RING, RING, RING, *piece), SUM),
            pltpu.VMEM((steps, own_blocks, RING, quarter, cases), SUM),
            pltpu.VMEM(plane, bf16),
            pltpu.VMEM(plane, bf16),
            pltpu.VMEM((steps, own_blocks, width, cases), bf16),
            pltpu.VMEM((steps, own_blocks, RING, quarter, cases), SUM),
            pltpu.VMEM((3, steps, *piece), SUM),
            pltpu.VMEM((steps, 3, *piece), SUM),
            *coded(halves), *coded(fulls), *coded(halves), *coded(fulls),
            *coded(direct), *coded(direct),
            pltpu.SemaphoreType.DMA((copies,)),
            pltpu.SemaphoreType.DMA((copies,)),
            pltpu.SemaphoreType.DMA((steps + 1, RING)),
        ],
        compiler_params=pltpu.CompilerParams(
            collective_id=0, has_side_effects=True, vmem_limit_bytes=60 * 2**20
        ),
    )(part, own, retarded, columns, inverse)


def local(strengths, incident_green, targets, history, retarded, columns, inverse):
    own_rows = history.shape[1]
    cases = history.shape[2]
    width = inverse.shape[1]
    own_blocks = inverse.shape[0]
    steps = strengths.shape[1] // cases
    part = incident_partial(strengths, incident_green, targets, own_blocks, steps)
    part = part.reshape(steps, 2, RING, RING, RING, own_blocks, width // RING, cases)
    blocked = (history.shape[0], own_blocks, width, cases)
    solved = march(part, history.reshape(blocked), retarded, columns, inverse, steps)
    return solved.reshape(steps, own_rows, cases)


def solution(mesh):
    placed = (
        P(("panel", "lag"), None),
        P(("panel", "lag"), None, None),
        P(("panel", "lag")),
        P("lag", "panel", None),
        P("lag", "panel", None, None, None),
        P("lag", "panel", None),
        P("panel", None, None),
    )
    return jax.shard_map(
        local, mesh=mesh, in_specs=placed, out_specs=P(None, "panel", None), check_vma=False
    )
```

```python
import functools

import jax
import jax.numpy as jnp
from jax import lax
from jax.experimental import pallas as pl
from jax.experimental.pallas import tpu as pltpu
from jax.sharding import PartitionSpec as P

MESH = pl.DeviceIdType.MESH
RING = 4
SUM = jnp.float32
CODE = jnp.int16
CODES = 32767.0
TINY = 1e-33


def incident_kernel(per_cell, steps, targets, green, cells, out, total, sem):
    group = pl.program_id(0)
    width = green.shape[1]
    own_blocks = total.shape[3]
    quarter = width // RING

    @pl.when(group == 0)
    def clear():
        def one(i, carry):
            total[i // (RING * RING), i % (RING * RING)] = jnp.zeros(total.shape[2:], SUM)
            return carry

        lax.fori_loop(0, steps * RING * RING, one, 0)

    def add_block(i, carry):
        target = targets[group * per_cell + i]
        device, block = target // own_blocks, target % own_blocks
        chip, core = device // 2, device % 2
        product = jnp.dot(green[i], cells[...], preferred_element_type=SUM)
        for s in range(steps):
            total[s, chip, core, block] += product[:, s * width : (s + 1) * width]
        return carry

    lax.fori_loop(0, per_cell, add_block, 0, unroll=per_cell)

    @pl.when(group == pl.num_programs(0) - 1)
    def store():
        copies = []
        for s in range(steps):
            for core in range(2):
                for j in range(RING):
                    copies.append(
                        pltpu.make_async_copy(
                            total.at[s, :, core, :, pl.ds(j * quarter, quarter)],
                            out.at[s, core, j],
                            sem.at[s, core, j],
                        )
                    )
        for copy in copies:
            copy.start()
        for copy in copies:
            copy.wait()


def incident_partial(strengths, green, targets, own_blocks, steps):
    count, width, _ = green.shape
    cell_blocks = strengths.shape[0] // width
    per_cell = count // cell_blocks
    chips = RING * RING
    return pl.pallas_call(
        functools.partial(incident_kernel, per_cell, steps),
        out_shape=jax.ShapeDtypeStruct(
            (steps, 2, RING, chips, own_blocks, width // RING, width), SUM
        ),
        grid_spec=pltpu.PrefetchScalarGridSpec(
            num_scalar_prefetch=1,
            grid=(cell_blocks,),
            in_specs=[
                pl.BlockSpec((per_cell, width, width), lambda g, t: (g, 0, 0)),
                pl.BlockSpec((width, strengths.shape[1]), lambda g, t: (g, 0)),
            ],
            out_specs=pl.BlockSpec(memory_space=pl.ANY),
            scratch_shapes=[
                pltpu.VMEM((steps, chips, 2, own_blocks, width, width), SUM),
                pltpu.SemaphoreType.DMA((steps, 2, RING)),
            ],
        ),
        compiler_params=pltpu.CompilerParams(vmem_limit_bytes=60 * 2**20),
    )(targets, green, strengths)


def add_into(target, *others):
    def one(i, carry):
        value = target[i]
        for other in others:
            value = value + other[i]
        target[i] = value
        return carry

    lax.fori_loop(0, target.shape[0], one, 0)


def scales_of(value):
    top = jnp.max(jnp.abs(value), axis=-2, keepdims=True)
    tiny = top < TINY
    return jnp.where(tiny, 0.0, CODES / jnp.where(tiny, 1.0, top)), jnp.where(tiny, 0.0, top * (1.0 / CODES))


def encode(source, codes, scales):
    def one(i, carry):
        value = source[i]
        there, back = scales_of(value)
        codes[i] = jnp.round(value * there).astype(jnp.int32).astype(codes.dtype)
        scales[i] = jnp.squeeze(back, -2)
        return carry

    lax.fori_loop(0, source.shape[0], one, 0)


def decode(codes, scales, i):
    return codes[i].astype(jnp.int32).astype(SUM) * jnp.expand_dims(scales[i], -2)


def add_decoded(target, *arrived):
    def one(i, carry):
        value = target[i]
        for codes, scales in arrived:
            value = value + decode(codes, scales, i)
        target[i] = value
        return carry

    lax.fori_loop(0, target.shape[0], one, 0)


def march_kernel(
    steps,
    part, own, retarded, columns, inverse, out,
    gath, gath_young, ret, quad, peer, base, new, newer, sols, aside, hsum, hgot, ygot,
    zhalf, zhalf_scale, zfull, zfull_scale, zhalf_out, zhalf_out_scale, zfull_out, zfull_out_scale,
    xgot, xgot_scale, xout, xout_scale,
    send_sems, recv_sems, local_sems,
):
    panel, z = lax.axis_index("panel"), lax.axis_index("lag")
    c, x, y = panel % 2, (panel // 2) % RING, panel // (2 * RING)
    lags, own_blocks, knz, width, _ = ret.shape
    quarter = width // RING
    others = (1, -1, 2)

    def hop(v, by):
        return lax.rem(v + (by + RING), RING)

    def at(yy, xx, cc):
        return (yy * RING + xx) * 2 + cc

    to_x = {d: (at(y, hop(x, d), c), z) for d in others}
    to_y = {d: (at(hop(y, d), x, c), z) for d in others}
    to_z = {d: (panel, hop(z, d)) for d in others}
    to_mate = (at(y, x, 1 - c), z)

    used = [0]

    def copy(src, dst, to):
        i = used[0]
        used[0] += 1
        return pltpu.make_async_remote_copy(
            src_ref=src, dst_ref=dst, send_sem=send_sems.at[i], recv_sem=recv_sems.at[i],
            device_id=to, device_id_type=MESH,
        )

    started = []

    def go(*copies):
        for one in copies:
            one.start()
            if not any(one is known for known in started):
                started.append(one)

    def only_start(*copies):
        for one in copies:
            one.start()

    def drain(n):
        for one in started[:n]:
            one.wait_send()
        del started[:n]

    def landed(*copies):
        for one in copies:
            one.wait_recv()

    class Gather:
        def __init__(self, view, go):
            whole = slice(None)
            self.go = go
            self.first, self.pass_on, self.wide, self.wide_on, self.mates = [], [], [], [], []
            for half, (near, far) in enumerate(((to_x, to_y), (to_y, to_x))):

                def spot(part, by, wide_by, half=half):
                    if half == 0:
                        return view(half, part, hop(y, wide_by), hop(x, by))
                    return view(half, part, hop(y, by), hop(x, wide_by))

                def line(wide_by, half=half):
                    return view(half, None, hop(y, wide_by), whole) if half == 0 else view(half, None, whole, hop(x, wide_by))

                def sent(part, by, wide_by, to):
                    return copy(spot(part, by, wide_by), spot(part, by, wide_by), to)

                self.first.append([sent(None, 0, 0, near[d]) for d in (1, -1)])
                self.pass_on.append([sent(0, -1, 0, near[1]), sent(1, 1, 0, near[-1])])
                self.wide.append({by: [sent(None, by, 0, far[d]) for d in (1, -1)] for by in (0, -1, 1, 2)})
                self.wide_on.append({by: [sent(0, by, -1, far[1]), sent(1, by, 1, far[-1])] for by in (0, -1, 1, 2)})
                self.mates.append([copy(line(by), line(by), to_mate) for by in (0, -1, 1, 2)])

        def start(self):
            for half in (0, 1):
                self.go(*self.first[half])
            for half in (0, 1):
                self.go(*self.wide[half][0])

        def pass_chunks(self):
            for d, by in ((0, -1), (1, 1)):
                for half in (0, 1):
                    landed(self.first[half][d])
                    self.go(self.pass_on[half][d])
            for by in (-1, 1):
                for half in (0, 1):
                    self.go(*self.wide[half][by])

        def far_chunk(self):
            for half in (0, 1):
                landed(*self.pass_on[half])
                self.go(*self.wide[half][2])
            for half in (0, 1):
                self.go(self.mates[half][0])

        def pass_wide(self, *which):
            for by in which:
                for d in (0, 1):
                    for half in (0, 1):
                        landed(self.wide[half][by][d])
                        self.go(self.wide_on[half][by][d])

        def pass_own(self):
            self.pass_wide(0)

        def pass_near(self):
            self.pass_wide(-1, 1)

        def pass_far(self):
            self.pass_wide(2)
            for d in (0, 1):
                for half in (0, 1):
                    self.go(self.mates[half][1 + d])

        def finish(self):
            for half in (0, 1):
                for by in (0, -1, 1, 2):
                    landed(*self.wide_on[half][by])
                self.go(self.mates[half][3])
            for half in (0, 1):
                landed(*self.mates[half])

        def wait_sends(self):
            for half in (0, 1):
                for group in (self.first, self.pass_on, self.mates, self.wide, self.wide_on):
                    members = group[half]
                    if isinstance(members, dict):
                        members = [one for pair in members.values() for one in pair]
                    for one in members:
                        one.wait_send()

    def halves_of(buffer, *front):
        def view(half, part, yy, xx):
            rows = width // 2
            first = half * rows
            if part is not None:
                rows = rows // 2
                first = first + part * rows
            return buffer.at[(*front, c, yy, xx, slice(None), pl.ds(first, rows))]

        return view

    past = Gather(halves_of(gath, slice(None)), go)
    between = used[0]
    young = Gather(halves_of(gath_young, slice(None)), only_start)
    used[0] = between
    spread = [Gather(halves_of(new), only_start)]
    used[0] = 0
    spread.append(Gather(halves_of(newer), only_start))
    used[0] = 2 * between
    younger = copy(own, gath_young.at[:, c, y, x], to_z[1])

    place, towards = {"z": z, "y": y, "x": x}, {"z": to_z, "y": to_y, "x": to_x}
    orders = ["zxy"] * (steps - 1) + ["yxz"]
    ordered = (2, 1, -1, 0)
    whole = slice(None)

    def cut(array, *front, **where):
        return array.at[(*front, *(where.get(axis, whole) for axis in "zyx"))]

    cores, kept = [], []
    for s, (a, _, _) in enumerate(orders):
        chunks = [{a: hop(place[a], by)} for by in ordered]
        cores.append([copy(cut(part, s, 1 - c, **at_chunk), cut(peer, s, **at_chunk), to_mate) for at_chunk in chunks])
        kept.append([
            pltpu.make_async_copy(cut(part, s, c, **at_chunk), cut(quad, s, **at_chunk), local_sems.at[s, i])
            for i, at_chunk in enumerate(chunks)
        ])
    matrices = pltpu.make_async_copy(retarded, ret, local_sems.at[steps, 0])

    def both(codes, scales, got, got_scales, to):
        return [copy(codes, got, to), copy(scales, got_scales, to)]

    ring_far, ring_free, ring_tied, second_all, third_all = [], [], [], [], []
    for s, (first, then, last) in enumerate(orders):
        to = towards[first]
        ring_far.append([
            both(zhalf_out.at[s, i], zhalf_out_scale.at[s, i], zhalf.at[s, i], zhalf_scale.at[s, i], to[d])
            for i, d in enumerate((1, -1))
        ])

        def near_half(i, h, s=s, to=to):
            rows = pl.ds(2 * h, 2)
            return both(
                zfull_out.at[s, i, rows], zfull_out_scale.at[s, i, rows], zfull.at[s, i, rows],
                zfull_scale.at[s, i, rows], to[(1, -1)[i]],
            )

        ring_free.append([near_half(i, 1 - i) for i in (0, 1)])
        ring_tied.append([near_half(i, i) for i in (0, 1)])
        second_all.append([
            both(xout.at[s, i], xout_scale.at[s, i], xgot.at[s, i], xgot_scale.at[s, i], towards[then][d])
            for i, d in enumerate(others)
        ])
        third_all.append([
            copy(
                cut(quad, s, **{first: place[first], then: place[then], last: hop(place[last], d)}),
                ygot.at[s, i], towards[last][d],
            )
            for i, d in enumerate(others)
        ])

    def ring_part(s, by, h=None):
        first, _, last = orders[s]
        where = {first: hop(place[first], by)}
        if h is not None:
            where[last] = pl.ds(2 * h, 2)
        return cut(quad, s, **where)

    def send_near(s, i, h, copies):
        rows = pl.ds(2 * h, 2)
        encode(ring_part(s, (1, -1)[i], h), zfull_out.at[s, i, rows], zfull_out_scale.at[s, i, rows])
        go(*copies)

    def over_cores(s, which=ordered):
        first = orders[s][0]
        for by in which:
            j = ordered.index(by)
            kept[s][j].wait()
            landed(cores[s][j])
            add_into(ring_part(s, by), cut(peer, s, **{first: hop(place[first], by)}))
            if by == 2:
                for i in (0, 1):
                    encode(ring_part(s, by, i), zhalf_out.at[s, i], zhalf_out_scale.at[s, i])
                    go(*ring_far[s][i])
            elif by:
                i = (1, -1).index(by)
                send_near(s, i, 1 - i, ring_free[s][i])

    def ring_pass(s):
        for i, d in enumerate((1, -1)):
            landed(*ring_far[s][i])
            add_decoded(ring_part(s, d, i), (zhalf.at[s, i], zhalf_scale.at[s, i]))
            send_near(s, i, i, ring_tied[s][i])

    def to_second(s):
        first, then, _ = orders[s]
        for i in (0, 1):
            landed(*ring_free[s][i], *ring_tied[s][i])
        add_decoded(ring_part(s, 0), *((zfull.at[s, i], zfull_scale.at[s, i]) for i in (0, 1)))
        for i, d in enumerate(others):
            encode(cut(quad, s, **{first: place[first], then: hop(place[then], d)}), xout.at[s, i], xout_scale.at[s, i])
            go(*second_all[s][i])

    def to_third(s):
        first, then, _ = orders[s]
        for one in second_all[s]:
            landed(*one)
        mine = cut(quad, s, **{first: place[first], then: place[then]})
        add_decoded(mine, *((xgot.at[s, i], xgot_scale.at[s, i]) for i in range(3)))
        go(*third_all[s])

    groups = [(s, 1) for s in range(steps)]
    older = [
        [
            copy(hsum.at[pl.ds(first, n), :, hop(z, d)], hgot.at[i, pl.ds(first, n)], to_z[d])
            for i, d in enumerate(others)
        ]
        for first, n in groups
    ]
    right = [[copy(base.at[s, :, z], base.at[s, :, z], to_z[d]) for d in others] for s in range(steps)]

    def right_side(s):
        landed(*third_all[s])
        total = quad[s, z, y, x] - hsum[s, :, z]
        for i in range(3):
            total = total + (ygot[s, i] - hgot[i, s])
        base[s, :, z] = total
        go(*right[s])

    told = {s: [[copy(sols.at[s, r], sols.at[s, r], to_z[d]) for r in range(own_blocks)] for d in others] for s in range(1, steps)}

    def field(buffer, front, col):
        chip = col // (2 * own_blocks)
        where = ((col // own_blocks) % 2, chip // RING, chip % RING, col % own_blocks)
        return buffer[(*front, *where)]

    def pairs(lag, r, fields):
        total = None
        for k in range(0, knz, 2):
            left = jnp.concatenate([ret[lag, r, k], ret[lag, r, k + 1]], 1)
            low = jnp.concatenate([fields(columns[r, lag, k]), fields(columns[r, lag, k + 1])], 0)
            product = jnp.dot(left, low, preferred_element_type=SUM)
            total = product if total is None else total + product
        return total

    def older_sums(first, n):
        def row(r, carry):
            total = None
            for lag in range(lags):

                def fields(col, lag=lag):
                    entries = [lag - s for s in range(first, first + n)]
                    found = [field(gath, (e,), col) if e >= 0 else field(gath_young, (lags + e,), col) for e in entries]
                    return jnp.concatenate(found, 1)

                value = pairs(lag, r, fields)
                total = value if total is None else total + value
            for j in range(n):
                hsum[first + j, r] = total[:, j * width : (j + 1) * width].reshape(RING, quarter, width)
            return carry

        lax.fori_loop(0, own_blocks, row, 0)

    def set_aside(lag, buffer):
        def row(r, carry):
            aside[r] = pairs(lag, r, lambda col: field(buffer, (), col))
            return carry

        lax.fori_loop(0, own_blocks, row, 0)

    def solve_row(s, r, buffer=None):
        rhs = base[s, r].reshape(width, width)
        if s == steps - 1:
            rhs = rhs - aside[r]
        if buffer is not None:
            rhs = rhs - pairs(0, r, lambda col: field(buffer, (), col))
        value = jnp.dot(inverse[r], rhs, precision=lax.Precision.HIGHEST, preferred_element_type=SUM)
        sols[s, r] = value.astype(sols.dtype)

    def solve(s, buffer=None):
        def row(r, carry):
            solve_row(s, r, buffer)
            return carry

        lax.fori_loop(0, own_blocks, row, 0)

    def leading(act):
        pl.when(z == 0)(act)

    def following(act):
        pl.when(z > 0)(act)

    barrier = pltpu.get_barrier_semaphore()
    neighbours = [*to_x.values(), *to_y.values(), *to_z.values(), to_mate]
    for to in neighbours:
        pl.semaphore_signal(barrier, inc=1, device_id=to, device_id_type=MESH)
    for pieces in kept:
        for k in pieces:
            k.start()
    matrices.start()
    gath[:, c, y, x] = own[...]
    pl.semaphore_wait(barrier, len(neighbours))

    go(*cores[0])
    past.start()
    pl.when(z < RING - 1)(younger.start)
    for pieces in cores[1:]:
        go(*pieces)

    def nothing_younger():
        def clear(i, carry):
            gath_young[i // (2 * RING), (i // RING) % 2, i % RING] = jnp.zeros(gath_young.shape[3:], gath_young.dtype)
            return carry

        lax.fori_loop(0, 4 * RING, clear, 0)

    leading(nothing_younger)

    def start_young():
        landed(younger)
        young.start()

    over_cores(0)
    past.pass_chunks()
    past.far_chunk()
    ring_pass(0)
    past.pass_own()
    over_cores(1)
    past.pass_near()
    past.pass_far()
    following(start_young)
    to_second(0)
    matrices.wait()
    past.finish()
    leading(lambda: over_cores(2, ordered[:1]))
    older_sums(*groups[0])
    go(*older[0])
    following(young.pass_chunks)
    to_third(0)
    leading(lambda: over_cores(2, ordered[1:]))
    following(young.far_chunk)
    landed(*older[0])
    ring_pass(1)
    right_side(0)
    following(young.pass_own)
    following(young.pass_near)
    leading(lambda: ring_pass(2))
    following(young.pass_far)
    to_second(1)
    landed(*right[0])
    solve(0)

    def send_first():
        new[c, y, x] = sols[0]
        spread[0].start()

    leading(send_first)
    following(lambda: over_cores(2))
    following(young.finish)
    older_sums(*groups[1])
    go(*older[1])
    leading(spread[0].pass_chunks)
    to_third(1)
    leading(spread[0].far_chunk)
    landed(*older[1])
    leading(spread[0].pass_own)
    leading(spread[0].pass_near)
    old = len(started)
    right_side(1)
    following(lambda: ring_pass(2))
    leading(spread[0].pass_far)
    leading(lambda: to_second(2))
    older_sums(*groups[2])
    drain(old)
    landed(*right[1])

    def second():
        spread[0].finish()
        solve(1, new)
        newer[c, y, x] = sols[1]
        spread[1].start()
        for pieces in told[1]:
            only_start(*pieces)

    leading(second)
    go(*older[2])
    following(lambda: to_second(2))
    leading(lambda: set_aside(1, new))
    to_third(2)
    leading(spread[1].pass_chunks)
    leading(spread[1].far_chunk)
    landed(*older[2])
    leading(spread[0].wait_sends)
    leading(spread[1].pass_own)
    leading(spread[1].pass_near)
    right_side(2)
    leading(spread[1].pass_far)
    landed(*right[2])

    def third():
        spread[1].finish()
        for r in range(own_blocks):
            solve_row(2, r, newer)
            only_start(*(pieces[r] for pieces in told[2]))
        spread[1].wait_sends()
        for s in range(1, steps):
            for pieces in told[s]:
                for one in pieces:
                    one.wait_send()

    leading(third)

    for i, d in enumerate(others):

        @pl.when(z == d % RING)
        def take(i=i):
            for s in range(1, steps):
                landed(*told[s][i])

    pl.when(z < RING - 1)(younger.wait_send)
    following(young.wait_sends)
    for one in started:
        one.wait_send()
    out[...] = sols[...]
    assert used[0] <= send_sems.shape[0], used[0]


def march(part, own, retarded, columns, inverse, steps):
    lags, own_blocks, knz, width, _ = retarded.shape
    quarter = width // RING
    cases = own.shape[-1]
    piece = (own_blocks, quarter, cases)
    line = (own_blocks, cases)
    bf16 = own.dtype
    plane = (2, RING, RING, own_blocks, width, cases)
    halves, fulls, direct = (steps, 2, RING // 2, RING), (steps, 2, RING, RING), (steps, 3, RING)

    def coded(lead):
        return [pltpu.VMEM((*lead, *piece), CODE), pltpu.VMEM((*lead, *line), SUM)]

    copies = 208
    return pl.pallas_call(
        functools.partial(march_kernel, steps),
        out_shape=jax.ShapeDtypeStruct((steps, own_blocks, width, cases), bf16),
        in_specs=[
            pl.BlockSpec(memory_space=pl.ANY),
            pl.BlockSpec(memory_space=pltpu.VMEM),
            pl.BlockSpec(memory_space=pl.ANY),
            pl.BlockSpec(memory_space=pltpu.SMEM),
            pl.BlockSpec(memory_space=pltpu.VMEM),
        ],
        out_specs=pl.BlockSpec(memory_space=pltpu.VMEM),
        scratch_shapes=[
            pltpu.VMEM((lags, *plane), bf16),
            pltpu.VMEM((lags, *plane), bf16),
            pltpu.VMEM(retarded.shape, bf16),
            pltpu.VMEM((steps, RING, RING, RING, *piece), SUM),
            pltpu.VMEM((steps, RING, RING, RING, *piece), SUM),
            pltpu.VMEM((steps, own_blocks, RING, quarter, cases), SUM),
            pltpu.VMEM(plane, bf16),
            pltpu.VMEM(plane, bf16),
            pltpu.VMEM((steps, own_blocks, width, cases), bf16),
            pltpu.VMEM((own_blocks, width, cases), SUM),
            pltpu.VMEM((steps, own_blocks, RING, quarter, cases), SUM),
            pltpu.VMEM((3, steps, *piece), SUM),
            pltpu.VMEM((steps, 3, *piece), SUM),
            *coded(halves), *coded(fulls), *coded(halves), *coded(fulls),
            *coded(direct), *coded(direct),
            pltpu.SemaphoreType.DMA((copies,)),
            pltpu.SemaphoreType.DMA((copies,)),
            pltpu.SemaphoreType.DMA((steps + 1, RING)),
        ],
        compiler_params=pltpu.CompilerParams(
            collective_id=0, has_side_effects=True, vmem_limit_bytes=60 * 2**20
        ),
    )(part, own, retarded, columns, inverse)


def local(strengths, incident_green, targets, history, retarded, columns, inverse):
    own_rows = history.shape[1]
    cases = history.shape[2]
    width = inverse.shape[1]
    own_blocks = inverse.shape[0]
    steps = strengths.shape[1] // cases
    part = incident_partial(strengths, incident_green, targets, own_blocks, steps)
    part = part.reshape(steps, 2, RING, RING, RING, own_blocks, width // RING, cases)
    blocked = (history.shape[0], own_blocks, width, cases)
    solved = march(part, history.reshape(blocked), retarded, columns.transpose(1, 0, 2), inverse, steps)
    return solved.reshape(steps, own_rows, cases)


def solution(mesh):
    placed = (
        P(("panel", "lag"), None),
        P(("panel", "lag"), None, None),
        P(("panel", "lag")),
        P("lag", "panel", None),
        P("lag", "panel", None, None, None),
        P("lag", "panel", None),
        P("panel", None, None),
    )
    return jax.shard_map(
        local, mesh=mesh, in_specs=placed, out_specs=P(None, "panel", None), check_vma=False
    )
```

```python
import functools

import jax
import jax.numpy as jnp
from jax import lax
from jax.experimental import pallas as pl
from jax.experimental.pallas import tpu as pltpu
from jax.sharding import PartitionSpec as P

MESH = pl.DeviceIdType.MESH
RING = 4
SUM = jnp.float32
CODE = jnp.int16
CODES = 32767.0
TINY = 1e-33


def incident_kernel(per_cell, steps, targets, green, cells, out, total, sem):
    group = pl.program_id(0)
    width = green.shape[1]
    own_blocks = total.shape[3]
    quarter = width // RING

    @pl.when(group == 0)
    def clear():
        def one(i, carry):
            total[i // (RING * RING), i % (RING * RING)] = jnp.zeros(total.shape[2:], SUM)
            return carry

        lax.fori_loop(0, steps * RING * RING, one, 0)

    def add_block(i, carry):
        target = targets[group * per_cell + i]
        device, block = target // own_blocks, target % own_blocks
        chip, core = device // 2, device % 2
        product = jnp.dot(green[i], cells[...], preferred_element_type=SUM)
        for s in range(steps):
            total[s, chip, core, block] += product[:, s * width : (s + 1) * width]
        return carry

    lax.fori_loop(0, per_cell, add_block, 0, unroll=per_cell)

    @pl.when(group == pl.num_programs(0) - 1)
    def store():
        copies = []
        for s in range(steps):
            for core in range(2):
                for j in range(RING):
                    copies.append(
                        pltpu.make_async_copy(
                            total.at[s, :, core, :, pl.ds(j * quarter, quarter)],
                            out.at[s, core, j],
                            sem.at[s, core, j],
                        )
                    )
        for copy in copies:
            copy.start()
        for copy in copies:
            copy.wait()


def incident_partial(strengths, green, targets, own_blocks, steps):
    count, width, _ = green.shape
    cell_blocks = strengths.shape[0] // width
    per_cell = count // cell_blocks
    chips = RING * RING
    return pl.pallas_call(
        functools.partial(incident_kernel, per_cell, steps),
        out_shape=jax.ShapeDtypeStruct(
            (steps, 2, RING, chips, own_blocks, width // RING, width), SUM
        ),
        grid_spec=pltpu.PrefetchScalarGridSpec(
            num_scalar_prefetch=1,
            grid=(cell_blocks,),
            in_specs=[
                pl.BlockSpec((per_cell, width, width), lambda g, t: (g, 0, 0)),
                pl.BlockSpec((width, strengths.shape[1]), lambda g, t: (g, 0)),
            ],
            out_specs=pl.BlockSpec(memory_space=pl.ANY),
            scratch_shapes=[
                pltpu.VMEM((steps, chips, 2, own_blocks, width, width), SUM),
                pltpu.SemaphoreType.DMA((steps, 2, RING)),
            ],
        ),
        compiler_params=pltpu.CompilerParams(vmem_limit_bytes=60 * 2**20),
    )(targets, green, strengths)


def add_into(target, *others):
    def one(i, carry):
        value = target[i]
        for other in others:
            value = value + other[i]
        target[i] = value
        return carry

    lax.fori_loop(0, target.shape[0], one, 0)


def scales_of(value):
    top = jnp.max(jnp.abs(value), axis=-2, keepdims=True)
    tiny = top < TINY
    return jnp.where(tiny, 0.0, CODES / jnp.where(tiny, 1.0, top)), jnp.where(tiny, 0.0, top * (1.0 / CODES))


def coded(value):
    there, back = scales_of(value)
    return jnp.round(value * there).astype(jnp.int32).astype(CODE), jnp.squeeze(back, -2)


def encode(source, codes, scales):
    def one(i, carry):
        codes[i], scales[i] = coded(source[i])
        return carry

    lax.fori_loop(0, source.shape[0], one, 0)


def decode(codes, scales, i):
    return codes[i].astype(jnp.int32).astype(SUM) * jnp.expand_dims(scales[i], -2)


def add_decoded(target, *arrived):
    def one(i, carry):
        value = target[i]
        for codes, scales in arrived:
            value = value + decode(codes, scales, i)
        target[i] = value
        return carry

    lax.fori_loop(0, target.shape[0], one, 0)


def march_kernel(
    steps,
    part, own, retarded, columns, inverse, out,
    gath, gath_young, ret, quad, peer, base, new, newer, sols, aside, hsum, hout, hout_scale, hgot, hgot_scale, rgot, rgot_scale,
    zhalf, zhalf_scale, zfull, zfull_scale, zhalf_out, zhalf_out_scale, zfull_out, zfull_out_scale,
    pgot, pgot_scale, pout, pout_scale,
    send_sems, recv_sems, local_sems,
):
    panel, z = lax.axis_index("panel"), lax.axis_index("lag")
    c, x, y = panel % 2, (panel // 2) % RING, panel // (2 * RING)
    lags, own_blocks, knz, width, _ = ret.shape
    quarter = width // RING
    others = (1, -1, 2)

    def hop(v, by):
        return lax.rem(v + (by + RING), RING)

    def at(yy, xx, cc):
        return (yy * RING + xx) * 2 + cc

    to_x = {d: (at(y, hop(x, d), c), z) for d in others}
    to_y = {d: (at(hop(y, d), x, c), z) for d in others}
    to_z = {d: (panel, hop(z, d)) for d in others}
    to_mate = (at(y, x, 1 - c), z)

    used = [0]

    def copy(src, dst, to):
        i = used[0]
        used[0] += 1
        return pltpu.make_async_remote_copy(
            src_ref=src, dst_ref=dst, send_sem=send_sems.at[i], recv_sem=recv_sems.at[i],
            device_id=to, device_id_type=MESH,
        )

    class Bundle:
        def __init__(self, pieces, got, sent=None):
            i = used[0]
            used[0] += 1

            def make(src, dst, to):
                return pltpu.make_async_remote_copy(
                    src_ref=src, dst_ref=dst, send_sem=send_sems.at[i], recv_sem=recv_sems.at[i],
                    device_id=to, device_id_type=MESH,
                )

            self.pieces = [make(*piece) for piece in pieces]
            sent = got if sent is None else sent
            self.got, self.sent = make(got, got, to_mate), make(sent, sent, to_mate)

        def start(self):
            for piece in self.pieces:
                piece.start()

        def wait_recv(self):
            self.got.wait_recv()

        def wait_send(self):
            self.sent.wait_send()

    started = []

    def go(*copies):
        for one in copies:
            one.start()
            if not any(one is known for known in started):
                started.append(one)

    def only_start(*copies):
        for one in copies:
            one.start()

    def drain(n):
        for one in started[:n]:
            one.wait_send()
        del started[:n]

    def landed(*copies):
        for one in copies:
            one.wait_recv()

    class Gather:
        def __init__(self, view, side, go):
            whole = slice(None)
            self.go = go
            self.first, self.pass_on, self.wide, self.wide_on, lines = [], [], [], [], []
            for half, (near, far) in enumerate(((to_x, to_y), (to_y, to_x))):

                def spot(part, by, wide_by, half=half):
                    if half == 0:
                        return view(half, part, hop(y, wide_by), hop(x, by))
                    return view(half, part, hop(y, by), hop(x, wide_by))

                def line(wide_by, half=half):
                    return view(half, None, hop(y, wide_by), whole) if half == 0 else view(half, None, whole, hop(x, wide_by))

                def sent(part, by, wide_by, to):
                    return copy(spot(part, by, wide_by), spot(part, by, wide_by), to)

                self.first.append([sent(None, 0, 0, near[d]) for d in (1, -1)])
                self.pass_on.append([sent(0, -1, 0, near[1]), sent(1, 1, 0, near[-1])])
                self.wide.append({by: [sent(None, by, 0, far[d]) for d in (1, -1)] for by in (0, -1, 1, 2)})
                self.wide_on.append({by: [sent(0, by, -1, far[1]), sent(1, by, 1, far[-1])] for by in (0, -1, 1, 2)})
                lines += [(line(by), line(by), to_mate) for by in (0, -1, 1, 2)]
            self.mates = Bundle(lines, side)

        def start(self):
            for half in (0, 1):
                self.go(*self.first[half])
            for half in (0, 1):
                self.go(*self.wide[half][0])

        def pass_chunks(self):
            for d, by in ((0, -1), (1, 1)):
                for half in (0, 1):
                    landed(self.first[half][d])
                    self.go(self.pass_on[half][d])
            for by in (-1, 1):
                for half in (0, 1):
                    self.go(*self.wide[half][by])

        def far_chunk(self):
            for half in (0, 1):
                landed(*self.pass_on[half])
                self.go(*self.wide[half][2])
            self.to_mates(0)

        def pass_wide(self, *which):
            for by in which:
                for d in (0, 1):
                    for half in (0, 1):
                        landed(self.wide[half][by][d])
                        self.go(self.wide_on[half][by][d])

        def pass_own(self):
            self.pass_wide(0)

        def pass_near(self):
            self.pass_wide(-1, 1)

        def pass_far(self):
            self.pass_wide(2)
            self.to_mates(1, 2)

        def finish(self):
            for half in (0, 1):
                for by in (0, -1, 1, 2):
                    landed(*self.wide_on[half][by])
            self.to_mates(3)
            landed(self.mates)

        def to_mates(self, *which):
            for i in which:
                for half in (0, 1):
                    self.mates.pieces[4 * half + i].start()

        def wait_sends(self):
            for half in (0, 1):
                for group in (self.first, self.pass_on, self.wide, self.wide_on):
                    members = group[half]
                    if isinstance(members, dict):
                        members = [one for pair in members.values() for one in pair]
                    for one in members:
                        one.wait_send()
            self.mates.wait_send()

    def halves_of(buffer, *front):
        def view(half, part, yy, xx):
            rows = width // 2
            first = half * rows
            if part is not None:
                rows = rows // 2
                first = first + part * rows
            return buffer.at[(*front, c, yy, xx, slice(None), pl.ds(first, rows))]

        return view

    past = Gather(halves_of(gath, slice(None)), gath.at[:, 0], only_start)
    between = used[0]
    young = Gather(halves_of(gath_young, slice(None)), gath_young.at[:, 0], only_start)
    used[0] = between
    spread = [Gather(halves_of(new), new.at[0], only_start)]
    used[0] = 0
    spread.append(Gather(halves_of(newer), newer.at[0], only_start))
    used[0] = 2 * between
    younger = copy(own, gath_young.at[:, c, y, x], to_z[1])

    place, towards = {"z": z, "y": y, "x": x}, {"z": to_z, "y": to_y, "x": to_x}
    orders = ["zxy"] * steps
    ordered = (2, 1, -1, 0)
    whole = slice(None)

    def cut(array, *front, **where):
        return array.at[(*front, *(where.get(axis, whole) for axis in "zyx"))]

    cores, kept = [], []
    for s, (a, _, _) in enumerate(orders):
        chunks = [{a: hop(place[a], by)} for by in ordered]
        cores.append([copy(cut(part, s, 1 - c, **at_chunk), cut(peer, s, **at_chunk), to_mate) for at_chunk in chunks])
        kept.append([
            pltpu.make_async_copy(cut(part, s, c, **at_chunk), cut(quad, s, **at_chunk), local_sems.at[s, i])
            for i, at_chunk in enumerate(chunks)
        ])
    matrices = pltpu.make_async_copy(retarded, ret, local_sems.at[steps, 0])

    def both(codes, scales, got, got_scales, to):
        return [copy(codes, got, to), copy(scales, got_scales, to)]

    near_by = [(dy, dx) for dy in (0, *others) for dx in (0, *others) if (dy, dx) != (0, 0)]
    ring_far, ring_free, ring_tied, over_plane = [], [], [], []
    for s, (first, then, last) in enumerate(orders):
        to = towards[first]
        ring_far.append([
            both(zhalf_out.at[s, i], zhalf_out_scale.at[s, i], zhalf.at[s, i], zhalf_scale.at[s, i], to[d])
            for i, d in enumerate((1, -1))
        ])

        def near_half(i, h, s=s, to=to):
            rows = pl.ds(2 * h, 2)
            return both(
                zfull_out.at[s, i, rows], zfull_out_scale.at[s, i, rows], zfull.at[s, i, rows],
                zfull_scale.at[s, i, rows], to[(1, -1)[i]],
            )

        ring_free.append([near_half(i, 1 - i) for i in (0, 1)])
        ring_tied.append([near_half(i, i) for i in (0, 1)])
        if first == "z":
            codes, scales = [], []
            for i, (dy, dx) in enumerate(near_by):
                yy, xx = hop(y, dy), hop(x, dx)
                codes.append((pout.at[s, yy, xx], pgot.at[s, i], (at(yy, xx, c), z)))
                scales.append((pout_scale.at[s, yy, xx], pgot_scale.at[s, i], (at(yy, xx, c), z)))
            over_plane.append([Bundle(codes, pgot.at[s]), Bundle(scales, pgot_scale.at[s])])
    def ring_part(s, by, h=None):
        first, _, last = orders[s]
        where = {first: hop(place[first], by)}
        if h is not None:
            where[last] = pl.ds(2 * h, 2)
        return cut(quad, s, **where)

    def send_near(s, i, h, copies):
        rows = pl.ds(2 * h, 2)
        encode(ring_part(s, (1, -1)[i], h), zfull_out.at[s, i, rows], zfull_out_scale.at[s, i, rows])
        go(*copies)

    def over_cores(s, which=ordered):
        first = orders[s][0]
        for by in which:
            j = ordered.index(by)
            kept[s][j].wait()
            landed(cores[s][j])
            add_into(ring_part(s, by), cut(peer, s, **{first: hop(place[first], by)}))
            if by == 2:
                for i in (0, 1):
                    encode(ring_part(s, by, i), zhalf_out.at[s, i], zhalf_out_scale.at[s, i])
                    go(*ring_far[s][i])
            elif by:
                i = (1, -1).index(by)
                send_near(s, i, 1 - i, ring_free[s][i])

    def ring_pass(s):
        for i, d in enumerate((1, -1)):
            landed(*ring_far[s][i])
            add_decoded(ring_part(s, d, i), (zhalf.at[s, i], zhalf_scale.at[s, i]))
            send_near(s, i, i, ring_tied[s][i])

    def ring_end(s):
        for i in (0, 1):
            landed(*ring_free[s][i], *ring_tied[s][i])
        add_decoded(ring_part(s, 0), *((zfull.at[s, i], zfull_scale.at[s, i]) for i in (0, 1)))

    def to_plane(s):
        ring_end(s)
        encode(quad.at[s, z], pout.at[s], pout_scale.at[s])
        go(*over_plane[s])

    def along_z(out, got, arrived):
        return Bundle([(out(d), got(i), to_z[d]) for i, d in enumerate(others)], arrived)

    older, right = [], []
    for s in range(steps):
        older.append([
            along_z(lambda d, out=out: out.at[s, hop(z, d)], lambda i, got=got: got.at[s, i], got.at[s])
            for out, got in ((hout, hgot), (hout_scale, hgot_scale))
        ])
        right.append([
            along_z(lambda d, got=got: got.at[s, z], lambda i, got=got: got.at[s, z], got.at[s, pl.ds(0, 3)])
            for got in (rgot, rgot_scale)
        ])

    def older_out(s):
        hout[s], hout_scale[s] = coded(hsum[s])
        go(*older[s])

    def right_side(s):
        total = quad[s, z, y, x] - hsum[s, z]
        for i in range(3):
            total = total - decode(hgot.at[s], hgot_scale.at[s], i)
        landed(*over_plane[s])
        for i in range(len(near_by)):
            total = total + decode(pgot.at[s], pgot_scale.at[s], i)
        rgot[s, z], rgot_scale[s, z] = coded(total)
        go(*right[s])

    def right_here(s):
        landed(*right[s])
        for q in range(RING):
            base[s, :, q] = decode(rgot.at[s], rgot_scale.at[s], q)

    told = [
        Bundle([(sols.at[s, r], sols.at[s, r], to_z[d]) for r in range(own_blocks) for d in others], sols.at[s], sols)
        for s in range(1, steps)
    ]

    def field(buffer, front, col):
        chip = col // (2 * own_blocks)
        where = ((col // own_blocks) % 2, chip // RING, chip % RING, col % own_blocks)
        return buffer[(*front, *where)]

    def pairs(lag, r, fields):
        total = None
        for k in range(0, knz, 2):
            left = jnp.concatenate([ret[lag, r, k], ret[lag, r, k + 1]], 1)
            low = jnp.concatenate([fields(columns[r, lag, k]), fields(columns[r, lag, k + 1])], 0)
            product = jnp.dot(left, low, preferred_element_type=SUM)
            total = product if total is None else total + product
        return total

    def older_sums(s, which):
        def row(r, carry):
            total = None if which[-1] == lags - 1 else hsum[s, :, r].reshape(width, width)
            for lag in which:
                e = lag - s
                entry, buffer = (e, gath) if e >= 0 else (lags + e, gath_young)
                value = pairs(lag, r, lambda col, entry=entry, buffer=buffer: field(buffer, (entry,), col))
                total = value if total is None else total + value
            hsum[s, :, r] = total.reshape(RING, quarter, width)
            return carry

        lax.fori_loop(0, own_blocks, row, 0)

    def set_aside(lag, buffer):
        def row(r, carry):
            aside[r] = pairs(lag, r, lambda col: field(buffer, (), col))
            return carry

        lax.fori_loop(0, own_blocks, row, 0)

    def solve_row(s, r, buffer=None):
        rhs = base[s, r].reshape(width, width)
        if s == steps - 1:
            rhs = rhs - aside[r]
        if buffer is not None:
            rhs = rhs - pairs(0, r, lambda col: field(buffer, (), col))
        value = jnp.dot(inverse[r], rhs, precision=lax.Precision.HIGHEST, preferred_element_type=SUM)
        sols[s, r] = value.astype(sols.dtype)

    def solve(s, buffer=None):
        def row(r, carry):
            solve_row(s, r, buffer)
            return carry

        lax.fori_loop(0, own_blocks, row, 0)

    def leading(act):
        pl.when(z == 0)(act)

    def following(act):
        pl.when(z > 0)(act)

    barrier = pltpu.get_barrier_semaphore()
    neighbours = [(at(hop(y, dy), hop(x, dx), c), z) for dy, dx in near_by] + [*to_z.values(), to_mate]
    for to in neighbours:
        pl.semaphore_signal(barrier, inc=1, device_id=to, device_id_type=MESH)
    for pieces in kept:
        for k in pieces:
            k.start()
    matrices.start()
    gath[:, c, y, x] = own[...]
    pl.semaphore_wait(barrier, len(neighbours))

    go(*cores[0])
    past.start()
    pl.when(z < RING - 1)(younger.start)
    for pieces in cores[1:]:
        go(*pieces)

    def nothing_younger():
        def clear(i, carry):
            gath_young[i // (2 * RING), (i // RING) % 2, i % RING] = jnp.zeros(gath_young.shape[3:], gath_young.dtype)
            return carry

        lax.fori_loop(0, 4 * RING, clear, 0)

    leading(nothing_younger)

    def start_young():
        landed(younger)
        young.start()

    over_cores(0)
    past.pass_chunks()
    past.far_chunk()
    ring_pass(0)
    past.pass_own()
    over_cores(1)
    past.pass_near()
    past.pass_far()
    following(start_young)
    to_plane(0)
    matrices.wait()
    past.finish()
    older_sums(0, range(lags))
    older_out(0)
    following(young.pass_chunks)
    older_sums(1, range(1, lags))
    landed(*older[0])
    right_side(0)
    ring_pass(1)
    following(young.far_chunk)
    following(young.pass_own)
    following(young.pass_near)
    old = len(started)
    over_cores(2)
    following(young.pass_far)
    right_here(0)
    solve(0)

    def send_first():
        new[c, y, x] = sols[0]
        spread[0].start()

    leading(send_first)
    leading(spread[0].pass_chunks)
    to_plane(1)
    following(young.finish)
    older_sums(1, range(1))
    older_out(1)
    leading(spread[0].far_chunk)
    ring_pass(2)
    older_sums(2, range(lags))
    landed(*older[1])
    right_side(1)
    older_out(2)
    leading(spread[0].pass_own)
    leading(spread[0].pass_near)
    leading(spread[0].pass_far)
    drain(old)
    past.wait_sends()
    to_plane(2)
    right_here(1)

    def second():
        spread[0].finish()
        solve(1, new)
        newer[c, y, x] = sols[1]
        spread[1].start()
        told[0].start()

    leading(second)
    leading(lambda: set_aside(1, new))
    leading(spread[1].pass_chunks)
    leading(spread[1].far_chunk)
    landed(*older[2])
    leading(spread[0].wait_sends)
    leading(spread[1].pass_own)
    leading(spread[1].pass_near)
    leading(spread[1].pass_far)
    right_side(2)
    right_here(2)

    def third():
        spread[1].finish()
        for r in range(own_blocks):
            solve_row(2, r, newer)
            only_start(*told[1].pieces[3 * r : 3 * r + 3])
        spread[1].wait_sends()
        for one in told:
            one.wait_send()

    leading(third)

    following(lambda: landed(*told))
    pl.when(z < RING - 1)(younger.wait_send)
    following(young.wait_sends)
    for one in started:
        one.wait_send()
    out[...] = sols[...]
    assert used[0] <= send_sems.shape[0], used[0]


def march(part, own, retarded, columns, inverse, steps):
    lags, own_blocks, knz, width, _ = retarded.shape
    quarter = width // RING
    cases = own.shape[-1]
    piece = (own_blocks, quarter, cases)
    line = (own_blocks, cases)
    bf16 = own.dtype
    plane = (2, RING, RING, own_blocks, width, cases)
    halves, fulls = (steps, 2, RING // 2, RING), (steps, 2, RING, RING)

    def parcels(lead):
        return [pltpu.VMEM((*lead, *piece), CODE), pltpu.VMEM((*lead, *line), SUM)]

    copies = 151
    return pl.pallas_call(
        functools.partial(march_kernel, steps),
        out_shape=jax.ShapeDtypeStruct((steps, own_blocks, width, cases), bf16),
        in_specs=[
            pl.BlockSpec(memory_space=pl.ANY),
            pl.BlockSpec(memory_space=pltpu.VMEM),
            pl.BlockSpec(memory_space=pl.ANY),
            pl.BlockSpec(memory_space=pltpu.SMEM),
            pl.BlockSpec(memory_space=pltpu.VMEM),
        ],
        out_specs=pl.BlockSpec(memory_space=pltpu.VMEM),
        scratch_shapes=[
            pltpu.VMEM((lags, *plane), bf16),
            pltpu.VMEM((lags, *plane), bf16),
            pltpu.VMEM(retarded.shape, bf16),
            pltpu.VMEM((steps, RING, RING, RING, *piece), SUM),
            pltpu.VMEM((steps, RING, RING, RING, *piece), SUM),
            pltpu.VMEM((steps, own_blocks, RING, quarter, cases), SUM),
            pltpu.VMEM(plane, bf16),
            pltpu.VMEM(plane, bf16),
            pltpu.VMEM((steps, own_blocks, width, cases), bf16),
            pltpu.VMEM((own_blocks, width, cases), SUM),
            pltpu.VMEM((steps, RING, *piece), SUM),
            *parcels((steps, RING)), *parcels((steps, 3)), *parcels((steps, RING)),
            *parcels(halves), *parcels(fulls), *parcels(halves), *parcels(fulls),
            *parcels((steps, RING * RING - 1)), *parcels((steps, RING, RING)),
            pltpu.SemaphoreType.DMA((copies,)),
            pltpu.SemaphoreType.DMA((copies,)),
            pltpu.SemaphoreType.DMA((steps + 1, RING)),
        ],
        compiler_params=pltpu.CompilerParams(
            collective_id=0, has_side_effects=True, vmem_limit_bytes=60 * 2**20
        ),
    )(part, own, retarded, columns, inverse)


def local(strengths, incident_green, targets, history, retarded, columns, inverse):
    own_rows = history.shape[1]
    cases = history.shape[2]
    width = inverse.shape[1]
    own_blocks = inverse.shape[0]
    steps = strengths.shape[1] // cases
    part = incident_partial(strengths, incident_green, targets, own_blocks, steps)
    part = part.reshape(steps, 2, RING, RING, RING, own_blocks, width // RING, cases)
    blocked = (history.shape[0], own_blocks, width, cases)
    solved = march(part, history.reshape(blocked), retarded, columns.transpose(1, 0, 2), inverse, steps)
    return solved.reshape(steps, own_rows, cases)


def solution(mesh):
    placed = (
        P(("panel", "lag"), None),
        P(("panel", "lag"), None, None),
        P(("panel", "lag")),
        P("lag", "panel", None),
        P("lag", "panel", None, None, None),
        P("lag", "panel", None),
        P("panel", None, None),
    )
    return jax.shard_map(
        local, mesh=mesh, in_specs=placed, out_specs=P(None, "panel", None), check_vma=False
    )
```

```python
import functools

import jax
import jax.numpy as jnp
from jax import lax
from jax.experimental import pallas as pl
from jax.experimental.pallas import tpu as pltpu
from jax.sharding import PartitionSpec as P

MESH = pl.DeviceIdType.MESH
RING = 4
SUM = jnp.float32
CODE = jnp.int16
CODES = 32767.0
TINY = 1e-33


def incident_kernel(per_cell, steps, targets, green, cells, out, total, sem):
    group = pl.program_id(0)
    width = green.shape[1]
    own_blocks = total.shape[3]
    quarter = width // RING

    @pl.when(group == 0)
    def clear():
        def one(i, carry):
            total[i // (RING * RING), i % (RING * RING)] = jnp.zeros(total.shape[2:], SUM)
            return carry

        lax.fori_loop(0, steps * RING * RING, one, 0)

    def add_block(i, carry):
        target = targets[group * per_cell + i]
        device, block = target // own_blocks, target % own_blocks
        chip, core = device // 2, device % 2
        product = jnp.dot(green[i], cells[...], preferred_element_type=SUM)
        for s in range(steps):
            total[s, chip, core, block] += product[:, s * width : (s + 1) * width]
        return carry

    lax.fori_loop(0, per_cell, add_block, 0, unroll=per_cell)

    @pl.when(group == pl.num_programs(0) - 1)
    def store():
        copies = []
        for s in range(steps):
            for core in range(2):
                for j in range(RING):
                    copies.append(
                        pltpu.make_async_copy(
                            total.at[s, :, core, :, pl.ds(j * quarter, quarter)],
                            out.at[s, core, j],
                            sem.at[s, core, j],
                        )
                    )
        for copy in copies:
            copy.start()
        for copy in copies:
            copy.wait()


def incident_partial(strengths, green, targets, own_blocks, steps):
    count, width, _ = green.shape
    cell_blocks = strengths.shape[0] // width
    per_cell = count // cell_blocks
    chips = RING * RING
    return pl.pallas_call(
        functools.partial(incident_kernel, per_cell, steps),
        out_shape=jax.ShapeDtypeStruct(
            (steps, 2, RING, chips, own_blocks, width // RING, width), SUM
        ),
        grid_spec=pltpu.PrefetchScalarGridSpec(
            num_scalar_prefetch=1,
            grid=(cell_blocks,),
            in_specs=[
                pl.BlockSpec((per_cell, width, width), lambda g, t: (g, 0, 0)),
                pl.BlockSpec((width, strengths.shape[1]), lambda g, t: (g, 0)),
            ],
            out_specs=pl.BlockSpec(memory_space=pl.ANY),
            scratch_shapes=[
                pltpu.VMEM((steps, chips, 2, own_blocks, width, width), SUM),
                pltpu.SemaphoreType.DMA((steps, 2, RING)),
            ],
        ),
        compiler_params=pltpu.CompilerParams(vmem_limit_bytes=60 * 2**20),
    )(targets, green, strengths)


def add_into(target, *others):
    def one(i, carry):
        value = target[i]
        for other in others:
            value = value + other[i]
        target[i] = value
        return carry

    lax.fori_loop(0, target.shape[0], one, 0)


def scales_of(value):
    top = jnp.max(jnp.abs(value), axis=-2, keepdims=True)
    tiny = top < TINY
    return jnp.where(tiny, 0.0, CODES / jnp.where(tiny, 1.0, top)), jnp.where(tiny, 0.0, top * (1.0 / CODES))


def coded(value):
    there, back = scales_of(value)
    return jnp.round(value * there).astype(jnp.int32).astype(CODE), jnp.squeeze(back, -2)


def encode(source, codes, scales):
    def one(i, carry):
        codes[i], scales[i] = coded(source[i])
        return carry

    lax.fori_loop(0, source.shape[0], one, 0)


def decode(codes, scales, i):
    return codes[i].astype(jnp.int32).astype(SUM) * jnp.expand_dims(scales[i], -2)


def add_decoded(target, *arrived):
    def one(i, carry):
        value = target[i]
        for codes, scales in arrived:
            value = value + decode(codes, scales, i)
        target[i] = value
        return carry

    lax.fori_loop(0, target.shape[0], one, 0)


def march_kernel(
    steps,
    part, own, retarded, columns, inverse, out,
    gath, gath_young, ret, quad, peer, base, new, newer, sols, aside, hsum, hout, hout_scale, hgot, hgot_scale, rgot, rgot_scale,
    zhalf, zhalf_scale, zfull, zfull_scale, zhalf_out, zhalf_out_scale, zfull_out, zfull_out_scale,
    pgot, pgot_scale, pout, pout_scale,
    send_sems, recv_sems, local_sems,
):
    panel, z = lax.axis_index("panel"), lax.axis_index("lag")
    c, x, y = panel % 2, (panel // 2) % RING, panel // (2 * RING)
    lags, own_blocks, knz, width, _ = ret.shape
    quarter = width // RING
    others = (1, -1, 2)

    def hop(v, by):
        return lax.rem(v + (by + RING), RING)

    def at(yy, xx, cc):
        return (yy * RING + xx) * 2 + cc

    to_x = {d: (at(y, hop(x, d), c), z) for d in others}
    to_y = {d: (at(hop(y, d), x, c), z) for d in others}
    to_z = {d: (panel, hop(z, d)) for d in others}
    to_mate = (at(y, x, 1 - c), z)

    used = [0]

    def copy(src, dst, to):
        i = used[0]
        used[0] += 1
        return pltpu.make_async_remote_copy(
            src_ref=src, dst_ref=dst, send_sem=send_sems.at[i], recv_sem=recv_sems.at[i],
            device_id=to, device_id_type=MESH,
        )

    class Bundle:
        def __init__(self, pieces, got, sent=None):
            i = used[0]
            used[0] += 1

            def make(src, dst, to):
                return pltpu.make_async_remote_copy(
                    src_ref=src, dst_ref=dst, send_sem=send_sems.at[i], recv_sem=recv_sems.at[i],
                    device_id=to, device_id_type=MESH,
                )

            self.pieces = [make(*piece) for piece in pieces]
            sent = got if sent is None else sent
            self.got, self.sent = make(got, got, to_mate), make(sent, sent, to_mate)

        def start(self):
            for piece in self.pieces:
                piece.start()

        def wait_recv(self):
            self.got.wait_recv()

        def wait_send(self):
            self.sent.wait_send()

    started = []

    def go(*copies):
        for one in copies:
            one.start()
            if not any(one is known for known in started):
                started.append(one)

    def only_start(*copies):
        for one in copies:
            one.start()

    def drain(n):
        for one in started[:n]:
            one.wait_send()
        del started[:n]

    def landed(*copies):
        for one in copies:
            one.wait_recv()

    class Gather:
        def __init__(self, view, side, go):
            whole = slice(None)
            self.go = go
            self.first, self.pass_on, self.wide, self.wide_on, lines = [], [], [], [], []
            for half, (near, far) in enumerate(((to_x, to_y), (to_y, to_x))):

                def spot(part, by, wide_by, half=half):
                    if half == 0:
                        return view(half, part, hop(y, wide_by), hop(x, by))
                    return view(half, part, hop(y, by), hop(x, wide_by))

                def line(wide_by, half=half):
                    return view(half, None, hop(y, wide_by), whole) if half == 0 else view(half, None, whole, hop(x, wide_by))

                def sent(part, by, wide_by, to):
                    return copy(spot(part, by, wide_by), spot(part, by, wide_by), to)

                self.first.append([sent(None, 0, 0, near[d]) for d in (1, -1)])
                self.pass_on.append([sent(0, -1, 0, near[1]), sent(1, 1, 0, near[-1])])
                self.wide.append({by: [sent(None, by, 0, far[d]) for d in (1, -1)] for by in (0, -1, 1, 2)})
                self.wide_on.append({by: [sent(0, by, -1, far[1]), sent(1, by, 1, far[-1])] for by in (0, -1, 1, 2)})
                lines += [(line(by), line(by), to_mate) for by in (0, -1, 1, 2)]
            self.mates = Bundle(lines, side)

        def start(self):
            for half in (0, 1):
                self.go(*self.first[half])
            for half in (0, 1):
                self.go(*self.wide[half][0])

        def pass_chunks(self):
            for d, by in ((0, -1), (1, 1)):
                for half in (0, 1):
                    landed(self.first[half][d])
                    self.go(self.pass_on[half][d])
            for by in (-1, 1):
                for half in (0, 1):
                    self.go(*self.wide[half][by])

        def far_chunk(self):
            for half in (0, 1):
                landed(*self.pass_on[half])
                self.go(*self.wide[half][2])
            self.to_mates(0)

        def pass_wide(self, *which):
            for by in which:
                for d in (0, 1):
                    for half in (0, 1):
                        landed(self.wide[half][by][d])
                        self.go(self.wide_on[half][by][d])

        def pass_own(self):
            self.pass_wide(0)

        def pass_near(self):
            self.pass_wide(-1, 1)

        def pass_far(self):
            self.pass_wide(2)
            self.to_mates(1, 2)

        def finish(self):
            for half in (0, 1):
                for by in (0, -1, 1, 2):
                    landed(*self.wide_on[half][by])
            self.to_mates(3)
            landed(self.mates)

        def to_mates(self, *which):
            for i in which:
                for half in (0, 1):
                    self.mates.pieces[4 * half + i].start()

        def wait_sends(self):
            for half in (0, 1):
                for group in (self.first, self.pass_on, self.wide, self.wide_on):
                    members = group[half]
                    if isinstance(members, dict):
                        members = [one for pair in members.values() for one in pair]
                    for one in members:
                        one.wait_send()
            self.mates.wait_send()

    def halves_of(buffer, *front):
        def view(half, part, yy, xx):
            rows = width // 2
            first = half * rows
            if part is not None:
                rows = rows // 2
                first = first + part * rows
            return buffer.at[(*front, c, yy, xx, slice(None), pl.ds(first, rows))]

        return view

    past = Gather(halves_of(gath, slice(None)), gath.at[:, 0], only_start)
    between = used[0]
    young = Gather(halves_of(gath_young, slice(None)), gath_young.at[:, 0], only_start)
    used[0] = between
    spread = [Gather(halves_of(new), new.at[0], only_start)]
    used[0] = 0
    spread.append(Gather(halves_of(newer), newer.at[0], only_start))
    used[0] = 2 * between
    younger = copy(own, gath_young.at[:, c, y, x], to_z[1])

    place, towards = {"z": z, "y": y, "x": x}, {"z": to_z, "y": to_y, "x": to_x}
    orders = ["zxy"] * steps
    ordered = (2, 1, -1, 0)
    whole = slice(None)

    def cut(array, *front, **where):
        return array.at[(*front, *(where.get(axis, whole) for axis in "zyx"))]

    cores, kept = [], []
    for s, (a, _, _) in enumerate(orders):
        chunks = [{a: hop(place[a], by)} for by in ordered]
        cores.append([copy(cut(part, s, 1 - c, **at_chunk), cut(peer, s, **at_chunk), to_mate) for at_chunk in chunks])
        kept.append([
            pltpu.make_async_copy(cut(part, s, c, **at_chunk), cut(quad, s, **at_chunk), local_sems.at[s, i])
            for i, at_chunk in enumerate(chunks)
        ])
    matrices = pltpu.make_async_copy(retarded, ret, local_sems.at[steps, 0])

    def both(codes, scales, got, got_scales, to):
        return [copy(codes, got, to), copy(scales, got_scales, to)]

    near_by = [(dy, dx) for dy in (0, *others) for dx in (0, *others) if (dy, dx) != (0, 0)]
    ring_far, ring_free, ring_tied, over_plane = [], [], [], []
    for s, (first, then, last) in enumerate(orders):
        to = towards[first]
        ring_far.append([
            both(zhalf_out.at[s, i], zhalf_out_scale.at[s, i], zhalf.at[s, i], zhalf_scale.at[s, i], to[d])
            for i, d in enumerate((1, -1))
        ])

        def near_half(i, h, s=s, to=to):
            rows = pl.ds(2 * h, 2)
            return both(
                zfull_out.at[s, i, rows], zfull_out_scale.at[s, i, rows], zfull.at[s, i, rows],
                zfull_scale.at[s, i, rows], to[(1, -1)[i]],
            )

        ring_free.append([near_half(i, 1 - i) for i in (0, 1)])
        ring_tied.append([near_half(i, i) for i in (0, 1)])
        if first == "z":
            codes, scales = [], []
            for i, (dy, dx) in enumerate(near_by):
                yy, xx = hop(y, dy), hop(x, dx)
                codes.append((pout.at[s, yy, xx], pgot.at[s, i], (at(yy, xx, c), z)))
                scales.append((pout_scale.at[s, yy, xx], pgot_scale.at[s, i], (at(yy, xx, c), z)))
            over_plane.append([Bundle(codes, pgot.at[s]), Bundle(scales, pgot_scale.at[s])])
    def ring_part(s, by, h=None):
        first, _, last = orders[s]
        where = {first: hop(place[first], by)}
        if h is not None:
            where[last] = pl.ds(2 * h, 2)
        return cut(quad, s, **where)

    def send_near(s, i, h, copies):
        rows = pl.ds(2 * h, 2)
        encode(ring_part(s, (1, -1)[i], h), zfull_out.at[s, i, rows], zfull_out_scale.at[s, i, rows])
        go(*copies)

    def over_cores(s, which=ordered):
        first = orders[s][0]
        for by in which:
            j = ordered.index(by)
            kept[s][j].wait()
            landed(cores[s][j])
            add_into(ring_part(s, by), cut(peer, s, **{first: hop(place[first], by)}))
            if by == 2:
                for i in (0, 1):
                    encode(ring_part(s, by, i), zhalf_out.at[s, i], zhalf_out_scale.at[s, i])
                    go(*ring_far[s][i])
            elif by:
                i = (1, -1).index(by)
                send_near(s, i, 1 - i, ring_free[s][i])

    def ring_pass(s):
        for i, d in enumerate((1, -1)):
            landed(*ring_far[s][i])
            add_decoded(ring_part(s, d, i), (zhalf.at[s, i], zhalf_scale.at[s, i]))
            send_near(s, i, i, ring_tied[s][i])

    def ring_end(s):
        for i in (0, 1):
            landed(*ring_free[s][i], *ring_tied[s][i])
        add_decoded(ring_part(s, 0), *((zfull.at[s, i], zfull_scale.at[s, i]) for i in (0, 1)))

    def to_plane(s):
        ring_end(s)
        encode(quad.at[s, z], pout.at[s], pout_scale.at[s])
        go(*over_plane[s])

    def along_z(out, got, arrived):
        return Bundle([(out(d), got(i), to_z[d]) for i, d in enumerate(others)], arrived)

    older, right = [], []
    for s in range(steps):
        older.append([
            along_z(lambda d, out=out: out.at[s, hop(z, d)], lambda i, got=got: got.at[s, i], got.at[s])
            for out, got in ((hout, hgot), (hout_scale, hgot_scale))
        ])
        right.append([
            along_z(lambda d, got=got: got.at[s, z], lambda i, got=got: got.at[s, z], got.at[s, pl.ds(0, 3)])
            for got in (rgot, rgot_scale)
        ])

    def older_out(s):
        hout[s], hout_scale[s] = coded(hsum[s])
        go(*older[s])

    def right_side(s):
        total = quad[s, z, y, x] - hsum[s, z]
        for i in range(3):
            total = total - decode(hgot.at[s], hgot_scale.at[s], i)
        landed(*over_plane[s])
        for i in range(len(near_by)):
            total = total + decode(pgot.at[s], pgot_scale.at[s], i)
        rgot[s, z], rgot_scale[s, z] = coded(total)
        go(*right[s])

    def right_here(s):
        landed(*right[s])
        for q in range(RING):
            base[s, :, q] = decode(rgot.at[s], rgot_scale.at[s], q)

    told = [
        Bundle([(sols.at[s, r], sols.at[s, r], to_z[d]) for r in range(own_blocks) for d in others], sols.at[s], sols)
        for s in range(1, steps)
    ]

    def field(buffer, front, col):
        chip = col // (2 * own_blocks)
        where = ((col // own_blocks) % 2, chip // RING, chip % RING, col % own_blocks)
        return buffer[(*front, *where)]

    def pairs(lag, r, fields):
        total = None
        for k in range(0, knz, 2):
            left = jnp.concatenate([ret[lag, r, k], ret[lag, r, k + 1]], 1)
            low = jnp.concatenate([fields(columns[r, lag, k]), fields(columns[r, lag, k + 1])], 0)
            product = jnp.dot(left, low, preferred_element_type=SUM)
            total = product if total is None else total + product
        return total

    def older_sums(s, which):
        def row(r, carry):
            total = None if which[-1] == lags - 1 else hsum[s, :, r].reshape(width, width)
            for lag in which:
                e = lag - s
                entry, buffer = (e, gath) if e >= 0 else (lags + e, gath_young)
                value = pairs(lag, r, lambda col, entry=entry, buffer=buffer: field(buffer, (entry,), col))
                total = value if total is None else total + value
            hsum[s, :, r] = total.reshape(RING, quarter, width)
            return carry

        lax.fori_loop(0, own_blocks, row, 0)

    def set_aside(lag, buffer):
        def row(r, carry):
            aside[r] = pairs(lag, r, lambda col: field(buffer, (), col))
            return carry

        lax.fori_loop(0, own_blocks, row, 0)

    def solve_row(s, r, buffer=None):
        rhs = base[s, r].reshape(width, width)
        if s == steps - 1:
            rhs = rhs - aside[r]
        if buffer is not None:
            rhs = rhs - pairs(0, r, lambda col: field(buffer, (), col))
        value = jnp.dot(inverse[r], rhs, precision=lax.Precision.HIGHEST, preferred_element_type=SUM)
        sols[s, r] = value.astype(sols.dtype)

    def solve(s, buffer=None):
        def row(r, carry):
            solve_row(s, r, buffer)
            return carry

        lax.fori_loop(0, own_blocks, row, 0)

    def leading(act):
        pl.when(z == 0)(act)

    def following(act):
        pl.when(z > 0)(act)

    barrier = pltpu.get_barrier_semaphore()
    neighbours = [(at(hop(y, dy), hop(x, dx), c), z) for dy, dx in near_by] + [*to_z.values(), to_mate]
    for to in neighbours:
        pl.semaphore_signal(barrier, inc=1, device_id=to, device_id_type=MESH)
    for pieces in kept:
        for k in pieces:
            k.start()
    matrices.start()
    gath[:, c, y, x] = own[...]
    pl.semaphore_wait(barrier, len(neighbours))

    go(*cores[0])
    past.start()
    pl.when(z < RING - 1)(younger.start)

    def nothing_younger():
        def clear(i, carry):
            gath_young[i // (2 * RING), (i // RING) % 2, i % RING] = jnp.zeros(gath_young.shape[3:], gath_young.dtype)
            return carry

        lax.fori_loop(0, 4 * RING, clear, 0)

    leading(nothing_younger)

    def start_young():
        landed(younger)
        young.start()

    over_cores(0)
    go(*cores[1])
    past.pass_chunks()
    past.far_chunk()
    ring_pass(0)
    past.pass_own()
    over_cores(1)
    go(*cores[2])
    past.pass_near()
    past.pass_far()
    following(start_young)
    to_plane(0)
    matrices.wait()
    past.finish()
    older_sums(0, range(lags))
    older_out(0)
    following(young.pass_chunks)
    older_sums(1, range(1, lags))
    landed(*older[0])
    right_side(0)
    ring_pass(1)
    following(young.far_chunk)
    following(young.pass_own)
    following(young.pass_near)
    old = len(started)
    over_cores(2)
    following(young.pass_far)
    right_here(0)
    solve(0)

    def send_first():
        new[c, y, x] = sols[0]
        spread[0].start()

    leading(send_first)
    leading(spread[0].pass_chunks)
    to_plane(1)
    following(young.finish)
    older_sums(1, range(1))
    older_out(1)
    leading(spread[0].far_chunk)
    ring_pass(2)
    older_sums(2, range(lags))
    landed(*older[1])
    right_side(1)
    older_out(2)
    leading(spread[0].pass_own)
    leading(spread[0].pass_near)
    leading(spread[0].pass_far)
    drain(old)
    past.wait_sends()
    to_plane(2)
    right_here(1)

    def second():
        spread[0].finish()
        solve(1, new)
        newer[c, y, x] = sols[1]
        spread[1].start()
        told[0].start()

    leading(second)
    leading(lambda: set_aside(1, new))
    leading(spread[1].pass_chunks)
    leading(spread[1].far_chunk)
    landed(*older[2])
    leading(spread[0].wait_sends)
    leading(spread[1].pass_own)
    leading(spread[1].pass_near)
    leading(spread[1].pass_far)
    right_side(2)
    right_here(2)

    def third():
        spread[1].finish()
        for r in range(own_blocks):
            solve_row(2, r, newer)
            only_start(*told[1].pieces[3 * r : 3 * r + 3])
        spread[1].wait_sends()
        for one in told:
            one.wait_send()

    leading(third)

    following(lambda: landed(*told))
    pl.when(z < RING - 1)(younger.wait_send)
    following(young.wait_sends)
    for one in started:
        one.wait_send()
    out[...] = sols[...]
    assert used[0] <= send_sems.shape[0], used[0]


def march(part, own, retarded, columns, inverse, steps):
    lags, own_blocks, knz, width, _ = retarded.shape
    quarter = width // RING
    cases = own.shape[-1]
    piece = (own_blocks, quarter, cases)
    line = (own_blocks, cases)
    bf16 = own.dtype
    plane = (2, RING, RING, own_blocks, width, cases)
    halves, fulls = (steps, 2, RING // 2, RING), (steps, 2, RING, RING)

    def parcels(lead):
        return [pltpu.VMEM((*lead, *piece), CODE), pltpu.VMEM((*lead, *line), SUM)]

    copies = 151
    return pl.pallas_call(
        functools.partial(march_kernel, steps),
        out_shape=jax.ShapeDtypeStruct((steps, own_blocks, width, cases), bf16),
        in_specs=[
            pl.BlockSpec(memory_space=pl.ANY),
            pl.BlockSpec(memory_space=pltpu.VMEM),
            pl.BlockSpec(memory_space=pl.ANY),
            pl.BlockSpec(memory_space=pltpu.SMEM),
            pl.BlockSpec(memory_space=pltpu.VMEM),
        ],
        out_specs=pl.BlockSpec(memory_space=pltpu.VMEM),
        scratch_shapes=[
            pltpu.VMEM((lags, *plane), bf16),
            pltpu.VMEM((lags, *plane), bf16),
            pltpu.VMEM(retarded.shape, bf16),
            pltpu.VMEM((steps, RING, RING, RING, *piece), SUM),
            pltpu.VMEM((steps, RING, RING, RING, *piece), SUM),
            pltpu.VMEM((steps, own_blocks, RING, quarter, cases), SUM),
            pltpu.VMEM(plane, bf16),
            pltpu.VMEM(plane, bf16),
            pltpu.VMEM((steps, own_blocks, width, cases), bf16),
            pltpu.VMEM((own_blocks, width, cases), SUM),
            pltpu.VMEM((steps, RING, *piece), SUM),
            *parcels((steps, RING)), *parcels((steps, 3)), *parcels((steps, RING)),
            *parcels(halves), *parcels(fulls), *parcels(halves), *parcels(fulls),
            *parcels((steps, RING * RING - 1)), *parcels((steps, RING, RING)),
            pltpu.SemaphoreType.DMA((copies,)),
            pltpu.SemaphoreType.DMA((copies,)),
            pltpu.SemaphoreType.DMA((steps + 1, RING)),
        ],
        compiler_params=pltpu.CompilerParams(
            collective_id=0, has_side_effects=True, vmem_limit_bytes=60 * 2**20
        ),
    )(part, own, retarded, columns, inverse)


def local(strengths, incident_green, targets, history, retarded, columns, inverse):
    own_rows = history.shape[1]
    cases = history.shape[2]
    width = inverse.shape[1]
    own_blocks = inverse.shape[0]
    steps = strengths.shape[1] // cases
    part = incident_partial(strengths, incident_green, targets, own_blocks, steps)
    part = part.reshape(steps, 2, RING, RING, RING, own_blocks, width // RING, cases)
    blocked = (history.shape[0], own_blocks, width, cases)
    solved = march(part, history.reshape(blocked), retarded, columns.transpose(1, 0, 2), inverse, steps)
    return solved.reshape(steps, own_rows, cases)


def solution(mesh):
    placed = (
        P(("panel", "lag"), None),
        P(("panel", "lag"), None, None),
        P(("panel", "lag")),
        P("lag", "panel", None),
        P("lag", "panel", None, None, None),
        P("lag", "panel", None),
        P("panel", None, None),
    )
    return jax.shard_map(
        local, mesh=mesh, in_specs=placed, out_specs=P(None, "panel", None), check_vma=False
    )
```

```python
import functools

import jax
import jax.numpy as jnp
from jax import lax
from jax.experimental import pallas as pl
from jax.experimental.pallas import tpu as pltpu
from jax.sharding import PartitionSpec as P

MESH = pl.DeviceIdType.MESH
RING = 4
SUM = jnp.float32
CODE = jnp.int16
CODES = 32767.0
TINY = 1e-33


def incident_kernel(per_cell, steps, targets, green, cells, out, total, sem):
    group = pl.program_id(0)
    width = green.shape[1]
    own_blocks = total.shape[3]
    quarter = width // RING

    @pl.when(group == 0)
    def clear():
        def one(i, carry):
            total[i // (RING * RING), i % (RING * RING)] = jnp.zeros(total.shape[2:], SUM)
            return carry

        lax.fori_loop(0, steps * RING * RING, one, 0)

    def add_block(i, carry):
        target = targets[group * per_cell + i]
        device, block = target // own_blocks, target % own_blocks
        chip, core = device // 2, device % 2
        product = jnp.dot(green[i], cells[...], preferred_element_type=SUM)
        for s in range(steps):
            total[s, chip, core, block] += product[:, s * width : (s + 1) * width]
        return carry

    lax.fori_loop(0, per_cell, add_block, 0, unroll=per_cell)

    @pl.when(group == pl.num_programs(0) - 1)
    def store():
        copies = []
        for s in range(steps):
            for core in range(2):
                for j in range(RING):
                    copies.append(
                        pltpu.make_async_copy(
                            total.at[s, :, core, :, pl.ds(j * quarter, quarter)],
                            out.at[s, core, j],
                            sem.at[s, core, j],
                        )
                    )
        for copy in copies:
            copy.start()
        for copy in copies:
            copy.wait()


def incident_partial(strengths, green, targets, own_blocks, steps):
    count, width, _ = green.shape
    cell_blocks = strengths.shape[0] // width
    per_cell = count // cell_blocks
    chips = RING * RING
    return pl.pallas_call(
        functools.partial(incident_kernel, per_cell, steps),
        out_shape=jax.ShapeDtypeStruct(
            (steps, 2, RING, chips, own_blocks, width // RING, width), SUM
        ),
        grid_spec=pltpu.PrefetchScalarGridSpec(
            num_scalar_prefetch=1,
            grid=(cell_blocks,),
            in_specs=[
                pl.BlockSpec((per_cell, width, width), lambda g, t: (g, 0, 0)),
                pl.BlockSpec((width, strengths.shape[1]), lambda g, t: (g, 0)),
            ],
            out_specs=pl.BlockSpec(memory_space=pl.ANY),
            scratch_shapes=[
                pltpu.VMEM((steps, chips, 2, own_blocks, width, width), SUM),
                pltpu.SemaphoreType.DMA((steps, 2, RING)),
            ],
        ),
        compiler_params=pltpu.CompilerParams(vmem_limit_bytes=60 * 2**20),
    )(targets, green, strengths)


def add_into(target, *others):
    def one(i, carry):
        value = target[i]
        for other in others:
            value = value + other[i]
        target[i] = value
        return carry

    lax.fori_loop(0, target.shape[0], one, 0)


def scales_of(value):
    top = jnp.max(jnp.abs(value), axis=-2, keepdims=True)
    tiny = top < TINY
    return jnp.where(tiny, 0.0, CODES / jnp.where(tiny, 1.0, top)), jnp.where(tiny, 0.0, top * (1.0 / CODES))


def coded(value):
    there, back = scales_of(value)
    return jnp.round(value * there).astype(jnp.int32).astype(CODE), jnp.squeeze(back, -2)


def encode(source, codes, scales):
    def one(i, carry):
        codes[i], scales[i] = coded(source[i])
        return carry

    lax.fori_loop(0, source.shape[0], one, 0)


def decode(codes, scales, i):
    return codes[i].astype(jnp.int32).astype(SUM) * jnp.expand_dims(scales[i], -2)


def add_decoded(target, *arrived):
    def one(i, carry):
        value = target[i]
        for codes, scales in arrived:
            value = value + decode(codes, scales, i)
        target[i] = value
        return carry

    lax.fori_loop(0, target.shape[0], one, 0)


def march_kernel(
    steps,
    part, own, retarded, columns, inverse, out,
    gath, gath_young, ret, quad, peer, base, new, newer, sols, aside, hsum, hout, hout_scale, hgot, hgot_scale, rgot, rgot_scale,
    zhalf, zhalf_scale, zfull, zfull_scale, zhalf_out, zhalf_out_scale, zfull_out, zfull_out_scale,
    pgot, pgot_scale, pout, pout_scale,
    send_sems, recv_sems, local_sems,
):
    panel, z = lax.axis_index("panel"), lax.axis_index("lag")
    c, x, y = panel % 2, (panel // 2) % RING, panel // (2 * RING)
    lags, own_blocks, knz, width, _ = ret.shape
    quarter = width // RING
    others = (1, -1, 2)

    def hop(v, by):
        return lax.rem(v + (by + RING), RING)

    def at(yy, xx, cc):
        return (yy * RING + xx) * 2 + cc

    to_x = {d: (at(y, hop(x, d), c), z) for d in others}
    to_y = {d: (at(hop(y, d), x, c), z) for d in others}
    to_z = {d: (panel, hop(z, d)) for d in others}
    to_mate = (at(y, x, 1 - c), z)

    used = [0]

    def copy(src, dst, to):
        i = used[0]
        used[0] += 1
        return pltpu.make_async_remote_copy(
            src_ref=src, dst_ref=dst, send_sem=send_sems.at[i], recv_sem=recv_sems.at[i],
            device_id=to, device_id_type=MESH,
        )

    class Bundle:
        def __init__(self, pieces, got, sent=None):
            i = used[0]
            used[0] += 1

            def make(src, dst, to):
                return pltpu.make_async_remote_copy(
                    src_ref=src, dst_ref=dst, send_sem=send_sems.at[i], recv_sem=recv_sems.at[i],
                    device_id=to, device_id_type=MESH,
                )

            self.pieces = [make(*piece) for piece in pieces]
            sent = got if sent is None else sent
            self.got, self.sent = make(got, got, to_mate), make(sent, sent, to_mate)

        def start(self):
            for piece in self.pieces:
                piece.start()

        def wait_recv(self):
            self.got.wait_recv()

        def wait_send(self):
            self.sent.wait_send()

    started = []

    def go(*copies):
        for one in copies:
            one.start()
            if not any(one is known for known in started):
                started.append(one)

    def only_start(*copies):
        for one in copies:
            one.start()

    def drain(n):
        for one in started[:n]:
            one.wait_send()
        del started[:n]

    def landed(*copies):
        for one in copies:
            one.wait_recv()

    class Gather:
        def __init__(self, view, side, row, go):
            whole = slice(None)
            self.go = go
            self.first, self.pass_on, self.wide, lines, onward = [], [], [], [], []
            for half, (near, far) in enumerate(((to_x, to_y), (to_y, to_x))):

                def spot(part, by, wide_by, half=half):
                    if half == 0:
                        return view(half, part, hop(y, wide_by), hop(x, by))
                    return view(half, part, hop(y, by), hop(x, wide_by))

                def line(wide_by, half=half):
                    return view(half, None, hop(y, wide_by), whole) if half == 0 else view(half, None, whole, hop(x, wide_by))

                def sent(part, by, wide_by, to):
                    return copy(spot(part, by, wide_by), spot(part, by, wide_by), to)

                self.first.append([sent(None, 0, 0, near[d]) for d in (1, -1)])
                self.pass_on.append([sent(0, -1, 0, near[1]), sent(1, 1, 0, near[-1])])
                self.wide.append({by: [sent(None, by, 0, far[d]) for d in (1, -1)] for by in (0, -1, 1, 2)})
                for by in (0, -1, 1, 2):
                    onward += [(spot(i, by, d), spot(i, by, d), far[-d]) for i, d in enumerate((-1, 1))]
                lines += [(line(by), line(by), to_mate) for by in (0, -1, 1, 2)]
            self.mates = Bundle(lines, side)
            self.wide_on = Bundle(onward, row)

        def start(self):
            for half in (0, 1):
                self.go(*self.first[half])
            for half in (0, 1):
                self.go(*self.wide[half][0])

        def pass_chunks(self):
            for d, by in ((0, -1), (1, 1)):
                for half in (0, 1):
                    landed(self.first[half][d])
                    self.go(self.pass_on[half][d])
            for by in (-1, 1):
                for half in (0, 1):
                    self.go(*self.wide[half][by])

        def far_chunk(self):
            for half in (0, 1):
                landed(*self.pass_on[half])
                self.go(*self.wide[half][2])
            self.to_mates(0)

        def pass_wide(self, *which):
            for by in which:
                for d in (0, 1):
                    for half in (0, 1):
                        landed(self.wide[half][by][d])
                        self.wide_on.pieces[8 * half + 2 * (0, -1, 1, 2).index(by) + d].start()

        def pass_own(self):
            self.pass_wide(0)

        def pass_near(self):
            self.pass_wide(-1, 1)

        def pass_far(self):
            self.pass_wide(2)
            self.to_mates(1, 2)

        def finish(self):
            landed(self.wide_on)
            self.to_mates(3)
            landed(self.mates)

        def to_mates(self, *which):
            for i in which:
                for half in (0, 1):
                    self.mates.pieces[4 * half + i].start()

        def wait_sends(self):
            for half in (0, 1):
                for group in (self.first, self.pass_on, self.wide):
                    members = group[half]
                    if isinstance(members, dict):
                        members = [one for pair in members.values() for one in pair]
                    for one in members:
                        one.wait_send()
            self.wide_on.wait_send()
            self.mates.wait_send()

    def halves_of(buffer, *front):
        def view(half, part, yy, xx):
            rows = width // 2
            first = half * rows
            if part is not None:
                rows = rows // 2
                first = first + part * rows
            return buffer.at[(*front, c, yy, xx, slice(None), pl.ds(first, rows))]

        return view

    past = Gather(halves_of(gath, slice(None)), gath.at[:, 0], gath.at[:, 0, 0], only_start)
    between = used[0]
    young = Gather(halves_of(gath_young, slice(None)), gath_young.at[:, 0], gath_young.at[:, 0, 0], only_start)
    used[0] = between
    spread = [Gather(halves_of(new), new.at[0], new.at[0, 0], only_start)]
    used[0] = 0
    spread.append(Gather(halves_of(newer), newer.at[0], newer.at[0, 0], only_start))
    used[0] = 2 * between
    younger = copy(own, gath_young.at[:, c, y, x], to_z[1])

    place, towards = {"z": z, "y": y, "x": x}, {"z": to_z, "y": to_y, "x": to_x}
    orders = ["zxy"] * steps
    ordered = (2, 1, -1, 0)
    whole = slice(None)

    def cut(array, *front, **where):
        return array.at[(*front, *(where.get(axis, whole) for axis in "zyx"))]

    cores, kept = [], []
    for s, (a, _, _) in enumerate(orders):
        chunks = [{a: hop(place[a], by)} for by in ordered]
        cores.append([copy(cut(part, s, 1 - c, **at_chunk), cut(peer, s, **at_chunk), to_mate) for at_chunk in chunks])
        kept.append([
            pltpu.make_async_copy(cut(part, s, c, **at_chunk), cut(quad, s, **at_chunk), local_sems.at[s, i])
            for i, at_chunk in enumerate(chunks)
        ])
    matrices = pltpu.make_async_copy(retarded, ret, local_sems.at[steps, 0])

    def both(codes, scales, got, got_scales, to):
        return [copy(codes, got, to), copy(scales, got_scales, to)]

    near_by = [(dy, dx) for dy in (0, *others) for dx in (0, *others) if (dy, dx) != (0, 0)]
    ring_far, ring_near, over_plane = [], [], []
    for s, (first, then, last) in enumerate(orders):
        to = towards[first]
        ring_far.append([
            both(zhalf_out.at[s, i], zhalf_out_scale.at[s, i], zhalf.at[s, i], zhalf_scale.at[s, i], to[d])
            for i, d in enumerate((1, -1))
        ])

        near = [(i, pl.ds(2 * h, 2), to[d]) for i, d in enumerate((1, -1)) for h in (0, 1)]
        ring_near.append([
            Bundle([(out.at[s, i, rows], got.at[s, i, rows], there) for i, rows, there in near], got.at[s])
            for out, got in ((zfull_out, zfull), (zfull_out_scale, zfull_scale))
        ])
        if first == "z":
            codes, scales = [], []
            for i, (dy, dx) in enumerate(near_by):
                yy, xx = hop(y, dy), hop(x, dx)
                codes.append((pout.at[s, yy, xx], pgot.at[s, i], (at(yy, xx, c), z)))
                scales.append((pout_scale.at[s, yy, xx], pgot_scale.at[s, i], (at(yy, xx, c), z)))
            over_plane.append([Bundle(codes, pgot.at[s]), Bundle(scales, pgot_scale.at[s])])
    def ring_part(s, by, h=None):
        first, _, last = orders[s]
        where = {first: hop(place[first], by)}
        if h is not None:
            where[last] = pl.ds(2 * h, 2)
        return cut(quad, s, **where)

    def send_near(s, i, h):
        rows = pl.ds(2 * h, 2)
        encode(ring_part(s, (1, -1)[i], h), zfull_out.at[s, i, rows], zfull_out_scale.at[s, i, rows])
        only_start(*(bundle.pieces[2 * i + h] for bundle in ring_near[s]))

    def over_cores(s, which=ordered):
        first = orders[s][0]
        for by in which:
            j = ordered.index(by)
            kept[s][j].wait()
            landed(cores[s][j])
            add_into(ring_part(s, by), cut(peer, s, **{first: hop(place[first], by)}))
            if by == 2:
                for i in (0, 1):
                    encode(ring_part(s, by, i), zhalf_out.at[s, i], zhalf_out_scale.at[s, i])
                    go(*ring_far[s][i])
            elif by:
                i = (1, -1).index(by)
                send_near(s, i, 1 - i)

    def ring_pass(s):
        for i, d in enumerate((1, -1)):
            landed(*ring_far[s][i])
            add_decoded(ring_part(s, d, i), (zhalf.at[s, i], zhalf_scale.at[s, i]))
            send_near(s, i, i)
        started.extend(ring_near[s])

    def ring_end(s):
        landed(*ring_near[s])
        add_decoded(ring_part(s, 0), *((zfull.at[s, i], zfull_scale.at[s, i]) for i in (0, 1)))

    def to_plane(s):
        ring_end(s)
        encode(quad.at[s, z], pout.at[s], pout_scale.at[s])
        go(*over_plane[s])

    def along_z(out, got, arrived):
        return Bundle([(out(d), got(i), to_z[d]) for i, d in enumerate(others)], arrived)

    older, right = [], []
    for s in range(steps):
        older.append([
            along_z(lambda d, out=out: out.at[s, hop(z, d)], lambda i, got=got: got.at[s, i], got.at[s])
            for out, got in ((hout, hgot), (hout_scale, hgot_scale))
        ])
        right.append([
            along_z(lambda d, got=got: got.at[s, z], lambda i, got=got: got.at[s, z], got.at[s, pl.ds(0, 3)])
            for got in (rgot, rgot_scale)
        ])

    def older_out(s):
        hout[s], hout_scale[s] = coded(hsum[s])
        go(*older[s])

    def right_side(s):
        total = quad[s, z, y, x] - hsum[s, z]
        for i in range(3):
            total = total - decode(hgot.at[s], hgot_scale.at[s], i)
        landed(*over_plane[s])
        for i in range(len(near_by)):
            total = total + decode(pgot.at[s], pgot_scale.at[s], i)
        rgot[s, z], rgot_scale[s, z] = coded(total)
        go(*right[s])

    def right_here(s):
        landed(*right[s])
        for q in range(RING):
            base[s, :, q] = decode(rgot.at[s], rgot_scale.at[s], q)

    told = [
        Bundle([(sols.at[s, r], sols.at[s, r], to_z[d]) for r in range(own_blocks) for d in others], sols.at[s], sols)
        for s in range(1, steps)
    ]

    def field(buffer, front, col):
        chip = col // (2 * own_blocks)
        where = ((col // own_blocks) % 2, chip // RING, chip % RING, col % own_blocks)
        return buffer[(*front, *where)]

    def pairs(lag, r, fields):
        total = None
        for k in range(0, knz, 2):
            left = jnp.concatenate([ret[lag, r, k], ret[lag, r, k + 1]], 1)
            low = jnp.concatenate([fields(columns[r, lag, k]), fields(columns[r, lag, k + 1])], 0)
            product = jnp.dot(left, low, preferred_element_type=SUM)
            total = product if total is None else total + product
        return total

    def older_sums(s, which):
        def row(r, carry):
            total = None if which[-1] == lags - 1 else hsum[s, :, r].reshape(width, width)
            for lag in which:
                e = lag - s
                entry, buffer = (e, gath) if e >= 0 else (lags + e, gath_young)
                value = pairs(lag, r, lambda col, entry=entry, buffer=buffer: field(buffer, (entry,), col))
                total = value if total is None else total + value
            hsum[s, :, r] = total.reshape(RING, quarter, width)
            return carry

        lax.fori_loop(0, own_blocks, row, 0)

    def set_aside(lag, buffer):
        def row(r, carry):
            aside[r] = pairs(lag, r, lambda col: field(buffer, (), col))
            return carry

        lax.fori_loop(0, own_blocks, row, 0)

    def solve_row(s, r, buffer=None):
        rhs = base[s, r].reshape(width, width)
        if s == steps - 1:
            rhs = rhs - aside[r]
        if buffer is not None:
            rhs = rhs - pairs(0, r, lambda col: field(buffer, (), col))
        value = jnp.dot(inverse[r], rhs, precision=lax.Precision.HIGHEST, preferred_element_type=SUM)
        sols[s, r] = value.astype(sols.dtype)

    def solve(s, buffer=None):
        def row(r, carry):
            solve_row(s, r, buffer)
            return carry

        lax.fori_loop(0, own_blocks, row, 0)

    def leading(act):
        pl.when(z == 0)(act)

    def following(act):
        pl.when(z > 0)(act)

    barrier = pltpu.get_barrier_semaphore()
    neighbours = [(at(hop(y, dy), hop(x, dx), c), z) for dy, dx in near_by] + [*to_z.values(), to_mate]
    for to in neighbours:
        pl.semaphore_signal(barrier, inc=1, device_id=to, device_id_type=MESH)
    for pieces in kept:
        for k in pieces:
            k.start()
    matrices.start()
    gath[:, c, y, x] = own[...]
    pl.semaphore_wait(barrier, len(neighbours))

    go(*cores[0])
    past.start()
    pl.when(z < RING - 1)(younger.start)
    for pieces in cores[1:]:
        go(*pieces)

    def nothing_younger():
        def clear(i, carry):
            gath_young[i // (2 * RING), (i // RING) % 2, i % RING] = jnp.zeros(gath_young.shape[3:], gath_young.dtype)
            return carry

        lax.fori_loop(0, 4 * RING, clear, 0)

    leading(nothing_younger)

    def start_young():
        landed(younger)
        young.start()

    over_cores(0)
    past.pass_chunks()
    past.far_chunk()
    ring_pass(0)
    past.pass_own()
    over_cores(1)
    past.pass_near()
    past.pass_far()
    following(start_young)
    to_plane(0)
    matrices.wait()
    past.finish()
    older_sums(0, range(lags))
    older_out(0)
    following(young.pass_chunks)
    older_sums(1, range(1, lags))
    landed(*older[0])
    right_side(0)
    ring_pass(1)
    following(young.far_chunk)
    following(young.pass_own)
    following(young.pass_near)
    old = len(started)
    over_cores(2)
    following(young.pass_far)
    right_here(0)
    solve(0)

    def send_first():
        new[c, y, x] = sols[0]
        spread[0].start()

    leading(send_first)
    leading(spread[0].pass_chunks)
    to_plane(1)
    following(young.finish)
    older_sums(1, range(1))
    older_out(1)
    leading(spread[0].far_chunk)
    ring_pass(2)
    older_sums(2, range(lags))
    landed(*older[1])
    right_side(1)
    older_out(2)
    leading(spread[0].pass_own)
    leading(spread[0].pass_near)
    leading(spread[0].pass_far)
    drain(old)
    past.wait_sends()
    to_plane(2)
    right_here(1)

    def second():
        spread[0].finish()
        solve(1, new)
        newer[c, y, x] = sols[1]
        spread[1].start()
        told[0].start()

    leading(second)
    leading(lambda: set_aside(1, new))
    leading(spread[1].pass_chunks)
    leading(spread[1].far_chunk)
    landed(*older[2])
    leading(spread[0].wait_sends)
    leading(spread[1].pass_own)
    leading(spread[1].pass_near)
    leading(spread[1].pass_far)
    right_side(2)
    right_here(2)

    def third():
        spread[1].finish()
        for r in range(own_blocks):
            solve_row(2, r, newer)
            only_start(*told[1].pieces[3 * r : 3 * r + 3])
        spread[1].wait_sends()
        for one in told:
            one.wait_send()

    leading(third)

    following(lambda: landed(*told))
    pl.when(z < RING - 1)(younger.wait_send)
    following(young.wait_sends)
    for one in started:
        one.wait_send()
    out[...] = sols[...]
    assert used[0] <= send_sems.shape[0], used[0]


def march(part, own, retarded, columns, inverse, steps):
    lags, own_blocks, knz, width, _ = retarded.shape
    quarter = width // RING
    cases = own.shape[-1]
    piece = (own_blocks, quarter, cases)
    line = (own_blocks, cases)
    bf16 = own.dtype
    plane = (2, RING, RING, own_blocks, width, cases)
    halves, fulls = (steps, 2, RING // 2, RING), (steps, 2, RING, RING)

    def parcels(lead):
        return [pltpu.VMEM((*lead, *piece), CODE), pltpu.VMEM((*lead, *line), SUM)]

    copies = 103
    return pl.pallas_call(
        functools.partial(march_kernel, steps),
        out_shape=jax.ShapeDtypeStruct((steps, own_blocks, width, cases), bf16),
        in_specs=[
            pl.BlockSpec(memory_space=pl.ANY),
            pl.BlockSpec(memory_space=pltpu.VMEM),
            pl.BlockSpec(memory_space=pl.ANY),
            pl.BlockSpec(memory_space=pltpu.SMEM),
            pl.BlockSpec(memory_space=pltpu.VMEM),
        ],
        out_specs=pl.BlockSpec(memory_space=pltpu.VMEM),
        scratch_shapes=[
            pltpu.VMEM((lags, *plane), bf16),
            pltpu.VMEM((lags, *plane), bf16),
            pltpu.VMEM(retarded.shape, bf16),
            pltpu.VMEM((steps, RING, RING, RING, *piece), SUM),
            pltpu.VMEM((steps, RING, RING, RING, *piece), SUM),
            pltpu.VMEM((steps, own_blocks, RING, quarter, cases), SUM),
            pltpu.VMEM(plane, bf16),
            pltpu.VMEM(plane, bf16),
            pltpu.VMEM((steps, own_blocks, width, cases), bf16),
            pltpu.VMEM((own_blocks, width, cases), SUM),
            pltpu.VMEM((steps, RING, *piece), SUM),
            *parcels((steps, RING)), *parcels((steps, 3)), *parcels((steps, RING)),
            *parcels(halves), *parcels(fulls), *parcels(halves), *parcels(fulls),
            *parcels((steps, RING * RING - 1)), *parcels((steps, RING, RING)),
            pltpu.SemaphoreType.DMA((copies,)),
            pltpu.SemaphoreType.DMA((copies,)),
            pltpu.SemaphoreType.DMA((steps + 1, RING)),
        ],
        compiler_params=pltpu.CompilerParams(
            collective_id=0, has_side_effects=True, vmem_limit_bytes=60 * 2**20
        ),
    )(part, own, retarded, columns, inverse)


def local(strengths, incident_green, targets, history, retarded, columns, inverse):
    own_rows = history.shape[1]
    cases = history.shape[2]
    width = inverse.shape[1]
    own_blocks = inverse.shape[0]
    steps = strengths.shape[1] // cases
    part = incident_partial(strengths, incident_green, targets, own_blocks, steps)
    part = part.reshape(steps, 2, RING, RING, RING, own_blocks, width // RING, cases)
    blocked = (history.shape[0], own_blocks, width, cases)
    solved = march(part, history.reshape(blocked), retarded, columns.transpose(1, 0, 2), inverse, steps)
    return solved.reshape(steps, own_rows, cases)


def solution(mesh):
    placed = (
        P(("panel", "lag"), None),
        P(("panel", "lag"), None, None),
        P(("panel", "lag")),
        P("lag", "panel", None),
        P("lag", "panel", None, None, None),
        P("lag", "panel", None),
        P("panel", None, None),
    )
    return jax.shard_map(
        local, mesh=mesh, in_specs=placed, out_specs=P(None, "panel", None), check_vma=False
    )
```
